256 devices in a mesh: tensor: 8 (over x, core), dp: 2 (over y_hi), replica: 16 (over z, y_lo).
Axes of the slice: x: 4, y: 4 (y_hi: 2, y_lo: 2; y = y_hi * 2 + y_lo), z: 8, core: 2. Of those that a mesh axis runs over, the one named last changes fastest.
Arguments:
- hidden_states: bfloat16 [16, 2, 512, 4096], P('replica', 'dp', 'tensor'), may hold values from -18 to 18, as said below
- grad_output: bfloat16 [16, 2, 512, 4096], P('replica', 'dp', 'tensor'), may hold values from -6 to 6
- w_in: bfloat16 [16, 4096, 6144], P('replica', None, 'tensor'), may hold values from -6 to 6
- w_out: bfloat16 [16, 4096, 4096], P('replica', 'tensor'), may hold values from -6 to 6
Outputs:
- input_grad: bfloat16 [16, 2, 512, 4096], P('replica', 'dp', 'tensor')
- synced_in: bfloat16 [4096, 6144], P(('dp', 'replica'), 'tensor')
- synced_out: bfloat16 [4096, 4096], P('tensor', ('dp', 'replica'))
The draws below stay inside these ranges and needn't reach their ends.
Inputs may be any that keep to these rules, and one draw needn't show every extreme that they name: `hidden_states`: each row holds one token's features.
All inputs are finite; a program needn't handle non-finite values.
Results may differ from the reference program's by a relative error of at most 0.028.
Values may be sent and summed in bfloat16 or wider, within the bound.
A program may use at most 128 MiB of HBM per device.

```python
import jax
import jax.numpy as jnp
from jax import lax

D = 4096
HQ = 32
HD = 128
SEQ = 512
REPLICAS = 16
NODE_DP = 2
QKV = 6144
N_TENSOR = 8


def draw_hidden_states(key, part):
    key = jax.random.fold_in(key, 7)
    noise_key = jax.random.fold_in(key, 0)
    full_shape = (REPLICAS, NODE_DP, SEQ, D)
    values = jax.random.truncated_normal(noise_key, -6.0, 6.0, full_shape, jnp.float32)
    return values.astype(jnp.bfloat16)


def raised(drawn, stream_key, source, target, shards_of, factor):
    def block_of(axis_at):
        return (jnp.arange(drawn.shape[axis_at]) // (drawn.shape[axis_at] // shards_of)).reshape((-1,) + (1,) * (drawn.ndim - 1 - axis_at))

    near = jax.random.permutation(stream_key, shards_of)[block_of(target)]
    second = (block_of(target) + shards_of // 2) % shards_of
    return jnp.where((block_of(source) == near) | (block_of(source) == second), factor * drawn, drawn)


def level_of(key, dims, cuts, least, largest):
    gain, own = 1.0, jax.random.fold_in(key, 6)
    for position, shards_of in cuts:
        draws = jnp.exp(jax.random.uniform(jax.random.fold_in(own, position), (shards_of,), jnp.float32, least / len(cuts), largest / len(cuts)))
        gain = gain * jnp.repeat(draws, dims[position] // shards_of).reshape([-1 if axis == position else 1 for axis in range(len(dims))])
    return gain


def centred(stream_key, extent, scale, bound, pieces=(), kind=jnp.bfloat16):
    gain = level_of(stream_key, extent, pieces, -0.22, 0.18) if pieces else 1.0
    entries = jax.random.normal(stream_key, extent, jnp.float32) * scale * gain
    return jnp.minimum(jnp.maximum(entries, -bound), bound).astype(kind)


def heavy_noise(key, shape, scale, reach, pieces, heavy, kind=jnp.bfloat16):
    drawn = scale * jax.random.normal(key, shape, jnp.float32)
    if pieces:
        drawn = drawn * level_of(key, shape, pieces, -0.22, 0.18)
    return jnp.clip(raised(drawn, jax.random.fold_in(key, 3), *heavy), -reach, reach).astype(kind)


def setup_inputs(seed: int = 0) -> dict:
    keys = jax.random.split(jax.random.key(seed), 5)
    hidden_states = draw_hidden_states(jax.random.fold_in(keys[4], 71), 0)
    grad_output = centred(keys[1], (REPLICAS, NODE_DP, SEQ, D), 1.0, 6.0, ((0, 16), (1, 2), (2, 8)))
    w_in = heavy_noise(keys[2], (REPLICAS, D, QKV), 1.0, 6.0, ((0, 16), (2, 8)), (0, 1, 16, 2.0))
    w_out = heavy_noise(keys[3], (REPLICAS, HQ * HD, D), 1.0, 6.0, ((0, 16), (1, 8)), (0, 2, 16, 2.0))
    return dict(hidden_states=hidden_states, grad_output=grad_output, w_in=w_in, w_out=w_out)


LEARN_RATE = 0.5
ROPE_BASE = 500000.0
MASK_VALUE = -1e30


def rope_tables(length, width):
    half_width = width // 2
    frequency = ROPE_BASE ** (-(jnp.arange(half_width, dtype=jnp.float32) * 2.0) / width)
    angles = jnp.arange(length, dtype=jnp.float32)[:, None] * frequency[None, :]
    cosine_table = jnp.concatenate([jnp.cos(angles), jnp.cos(angles)], axis=1)
    sine_table = jnp.concatenate([jnp.sin(angles), jnp.sin(angles)], axis=1)
    return cosine_table[:, None, :], sine_table[:, None, :]


def rotate(values, cosine_table, sine_table):
    half_width = values.shape[-1] // 2
    lower_half = values[..., :half_width]
    upper_half = values[..., half_width:]
    return values * cosine_table + jnp.concatenate([-upper_half, lower_half], -1) * sine_table


def unrotate(gradient, cosine_table, sine_table):
    half_width = gradient.shape[-1] // 2
    scaled = gradient * sine_table
    return gradient * cosine_table + jnp.concatenate([scaled[..., half_width:], -scaled[..., :half_width]], -1)


def widen(array):
    return array.astype(jnp.float32)


def local_backward(inputs, upstream, weight_in, weight_out):
    length = inputs.shape[0]
    out_width = weight_out.shape[0]
    heads_q = out_width // HD
    heads_kv = (weight_in.shape[1] - out_width) // (2 * HD)
    group_size = heads_q // heads_kv
    projected = jnp.dot(inputs, weight_in, preferred_element_type=jnp.float32) * D ** -0.5
    cosine_table, sine_table = rope_tables(length, HD)
    query_heads = rotate(projected[:, :out_width].reshape(length, heads_q, HD), cosine_table, sine_table).astype(jnp.bfloat16)
    key_heads = rotate(projected[:, out_width:out_width + heads_kv * HD].reshape(length, heads_kv, HD), cosine_table, sine_table).astype(jnp.bfloat16)
    value_heads = projected[:, out_width + heads_kv * HD:].reshape(length, heads_kv, HD).astype(jnp.bfloat16)
    query_groups = query_heads.reshape(length, heads_kv, group_size, HD)
    scores = jnp.einsum('skgd,tkd->kgst', widen(query_groups), widen(key_heads)) * HD ** -0.5
    causal = jnp.arange(length)[:, None] >= jnp.arange(length)[None, :]
    scores = jnp.where(causal, scores, MASK_VALUE)
    probabilities = jax.nn.softmax(scores, axis=-1)
    weights = probabilities.astype(jnp.bfloat16)
    context = jnp.einsum('kgst,tkd->skgd', widen(weights), widen(value_heads)).astype(jnp.bfloat16)
    dcontext = (jnp.dot(upstream, weight_out.T, preferred_element_type=jnp.float32) * (HQ * HD) ** -0.5).astype(jnp.bfloat16)
    dcontext_groups = dcontext.reshape(length, heads_kv, group_size, HD)
    dprobs = jnp.einsum('skgd,tkd->kgst', widen(dcontext_groups), widen(value_heads))
    dvalue = jnp.einsum('kgst,skgd->tkd', widen(weights), widen(dcontext_groups))
    row_delta = jnp.einsum('skgd,skgd->kgs', widen(dcontext_groups), widen(context))[..., None]
    dscores = (probabilities * (dprobs - row_delta) * HD ** -0.5).astype(jnp.bfloat16)
    dquery = jnp.einsum('kgst,tkd->skgd', widen(dscores), widen(key_heads)).reshape(length, heads_q, HD)
    key_grad = jnp.einsum('kgst,skgd->tkd', widen(dscores), widen(query_groups))
    dquery = unrotate(dquery, cosine_table, sine_table)
    key_grad = unrotate(key_grad, cosine_table, sine_table)
    dprojected = jnp.concatenate([dquery.reshape(length, -1), key_grad.reshape(length, -1), dvalue.reshape(length, -1)], 1).astype(jnp.bfloat16)
    return dprojected, context.reshape(length, out_width)


def reference(hidden_states, grad_output, w_in, w_out):
    block_in = w_in.shape[2] // N_TENSOR
    block_out = w_out.shape[1] // N_TENSOR
    scale_in = D ** -0.5
    scale_out = (HQ * HD) ** -0.5
    total_in = jnp.zeros((D, QKV), jnp.float32)
    total_out = jnp.zeros((HQ * HD, D), jnp.float32)
    input_grads = []
    for replica_index in range(REPLICAS):
        grad_in = jnp.zeros((D, QKV), jnp.float32)
        grad_out = jnp.zeros((HQ * HD, D), jnp.float32)
        row_blocks = []
        for node_index in range(NODE_DP):
            inputs = hidden_states[replica_index, node_index]
            upstream = grad_output[replica_index, node_index]
            partial_sum = jnp.zeros((SEQ, D), jnp.float32)
            in_blocks = []
            out_blocks = []
            for group_index in range(N_TENSOR):
                weight_in = w_in[replica_index, :, group_index * block_in:(group_index + 1) * block_in]
                weight_out = w_out[replica_index, group_index * block_out:(group_index + 1) * block_out]
                dprojected, context = local_backward(inputs, upstream, weight_in, weight_out)
                partial_value = (jnp.dot(dprojected, weight_in.T, preferred_element_type=jnp.float32) * scale_in).astype(jnp.bfloat16)
                partial_sum = partial_sum + lax.optimization_barrier(partial_value).astype(jnp.float32)
                in_blocks.append(jnp.dot(inputs.T, dprojected, preferred_element_type=jnp.float32) * scale_in)
                out_blocks.append(jnp.dot(context.T, upstream, preferred_element_type=jnp.float32) * scale_out)
            grad_in = grad_in + jnp.concatenate(in_blocks, 1)
            grad_out = grad_out + jnp.concatenate(out_blocks, 0)
            row_blocks.append(partial_sum.astype(jnp.bfloat16))
        input_grads.append(jnp.stack(row_blocks))
        total_in = total_in + (w_in[replica_index].astype(jnp.float32) - LEARN_RATE * grad_in) / REPLICAS
        total_out = total_out + (w_out[replica_index].astype(jnp.float32) - LEARN_RATE * grad_out) / REPLICAS
    return jnp.stack(input_grads), total_in.astype(jnp.bfloat16), total_out.astype(jnp.bfloat16)
```

```python
import functools

import jax
import jax.numpy as jnp
import numpy as np
from jax import lax
from jax.experimental import pallas as pl
from jax.experimental.pallas import tpu as pltpu
from jax.sharding import PartitionSpec as P

D = 4096
HQ = 32
HD = 128
SEQ = 512
REPLICAS = 16
NODE_DP = 2
LEARN_RATE = 0.5
ROPE_BASE = 500000.0
MASK_VALUE = -1e30

NX, NY, NZ = 4, 4, 8

HEADS = 4
QW = HEADS * HD
IN_W = QW + 2 * HD
TOK = 64
A_ROWS = QW // 2
B_COLS = IN_W // 2
X_COLS = D // 2
CHUNK = D // (NY * NZ)
SCALE_IN = D ** (-0.5)
SCALE_OUT = (HQ * HD) ** (-0.5)
SCALE_HD = HD ** (-0.5)
W_SHARE = 1.0 / (NODE_DP * REPLICAS)
G_IN = -LEARN_RATE * SCALE_IN / REPLICAS
G_OUT = -LEARN_RATE * SCALE_OUT / REPLICAS

BF16 = jnp.bfloat16
F32 = jnp.float32


def rope_tables():
    half = HD // 2
    frequency = np.float32(ROPE_BASE) ** (
        -(np.arange(half, dtype=np.float32) * np.float32(2.0)) / np.float32(HD)
    )
    angles = np.arange(SEQ, dtype=np.float32)[:, None] * frequency[None, :].astype(np.float32)
    cosine, sine = np.cos(angles).astype(np.float32), np.sin(angles).astype(np.float32)
    return np.concatenate([cosine, cosine], 1), np.concatenate([-sine, sine], 1)


def mm(left, right):
    return lax.dot_general(left, right, (((1,), (0,)), ((), ())), preferred_element_type=F32)


def mm_nt(left, right):
    return lax.dot_general(left, right, (((1,), (1,)), ((), ())), preferred_element_type=F32)


def mm_tn(left, right):
    return lax.dot_general(left, right, (((0,), (0,)), ((), ())), preferred_element_type=F32)


def body(
    hid, gout, w_in, w_out, cos_h, sin_h,
    ig_ref, sin_ref, sout_ref,
    H, G, HT, WI, WO, COS, SIN, Q, K, V, PR, C, CT, DC, DP, DK, DV,
    a0, ar, ao, b0, br, bo, PB, igr, x0, xr,
    lsem, ag_s, ag_r, a_s, a_r, ao_s, ao_r, b_s, b_r, bo_s, bo_r, sib_s, sib_r, x_s, x_r,
):
    t = lax.axis_index("tensor")
    x, core = t // 2, t % 2
    dp = lax.axis_index("dp")
    rep = lax.axis_index("replica")
    z, ylo = rep // 2, rep % 2
    y = dp * 2 + ylo

    def x_dev(step):
        return {"tensor": ((x + step + NX) % NX) * 2 + core}

    def y_dev(step):
        other = (y + step + NY) % NY
        return {"dp": other // 2, "replica": z * 2 + other % 2}

    def z_dev(step):
        return {"replica": ((z + step + NZ) % NZ) * 2 + ylo}

    sib = {"tensor": x * 2 + 1 - core}

    def remote(src, dst, ssem, rsem, dev):
        return pltpu.make_async_remote_copy(
            src_ref=src, dst_ref=dst, send_sem=ssem, recv_sem=rsem,
            device_id=dev, device_id_type=pl.DeviceIdType.MESH,
        )

    my_rows = pl.ds(pl.multiple_of((x * 2 + core) * TOK, TOK), TOK)
    loads = [
        pltpu.make_async_copy(hid.at[0, 0], H.at[my_rows], lsem.at[0]),
        pltpu.make_async_copy(gout.at[0, 0], G.at[my_rows], lsem.at[1]),
        pltpu.make_async_copy(cos_h, COS, lsem.at[2]),
        pltpu.make_async_copy(sin_h, SIN, lsem.at[3]),
        pltpu.make_async_copy(w_in.at[0], WI, lsem.at[4]),
        pltpu.make_async_copy(w_out.at[0], WO, lsem.at[5]),
    ]
    for load in loads:
        load.start()

    barrier = pltpu.get_barrier_semaphore()
    peers = [x_dev(1), x_dev(-1), sib, y_dev(1), y_dev(-1), z_dev(1), z_dev(-1)]
    for peer in peers:
        pl.semaphore_signal(barrier, inc=1, device_id=peer, device_id_type=pl.DeviceIdType.MESH)
    pl.semaphore_wait(barrier, len(peers))

    def gather(i, shard, full):
        def rows(step, start=0, size=TOK):
            at = (((x + step + NX) % NX) * 2 + core) * TOK + start
            return full.at[pl.ds(pl.multiple_of(at, 32), size)]

        def msg(m, src, dst, dev):
            return remote(src, dst, ag_s.at[i, m], ag_r.at[i, m], dev)

        half = TOK // 2
        own = shard.at[0, 0]
        return [
            msg(0, own, rows(0), x_dev(1)),
            msg(1, own, rows(0), x_dev(-1)),
            msg(2, own, rows(0), sib),
            msg(3, rows(-1, 0, half), rows(-1, 0, half), x_dev(1)),
            msg(4, rows(-1), rows(-1), sib),
            msg(5, rows(1, half, half), rows(1, half, half), x_dev(-1)),
            msg(6, rows(1), rows(1), sib),
            msg(7, rows(2, 0, half), rows(2, 0, half), sib),
            msg(8, rows(2, half, half), rows(2, half, half), sib),
        ]

    gh = gather(0, hid, H)
    gg = gather(1, gout, G)

    def first(msgs):
        for m in (0, 1, 2):
            msgs[m].start()

    def relay(msgs):
        msgs[0].wait_recv()
        msgs[3].start()
        msgs[1].wait_recv()
        msgs[5].start()
        msgs[4].start()
        msgs[6].start()

    def last(msgs):
        msgs[3].wait_recv()
        msgs[7].start()
        msgs[5].wait_recv()
        msgs[8].start()
        for m in (2, 4, 6, 7, 8):
            msgs[m].wait_recv()

    first(gh)
    relay(gh)
    first(gg)
    for load in loads[2:]:
        load.wait()
    loads[0].wait()
    last(gh)

    cosine, sine = COS, SIN

    def rotate(v):
        return v * cosine[...] + pltpu.roll(v, HD // 2, 1) * sine[...]

    def unrotate(g):
        return g * cosine[...] + pltpu.roll(g * sine[...], HD // 2, 1)

    for n in range(3):
        proj = mm(H[...], WI[:, n * 256 : n * 256 + 256]) * SCALE_IN
        left, right = proj[:, :HD], proj[:, HD:]
        if n < 2:
            Q[:, n * 256 : n * 256 + HD] = rotate(left).astype(BF16)
            Q[:, n * 256 + HD : n * 256 + 256] = rotate(right).astype(BF16)
        else:
            K[...] = rotate(left).astype(BF16)
            V[...] = right.astype(BF16)

    @pl.loop(0, D // 256)
    def _(n):
        at = pl.multiple_of(n * 256, 256)
        HT[pl.ds(at, 256), :] = H[:, pl.ds(at, 256)].T

    RB = 128

    @pl.loop(0, HEADS)
    def _(j):
        cols = pl.ds(pl.multiple_of(j * HD, HD), HD)
        for i in range(SEQ // RB):
            r, kx = i * RB, (i + 1) * RB
            s = mm_nt(Q[r : r + RB, cols], K[:kx, :]) * SCALE_HD
            row = lax.broadcasted_iota(jnp.int32, (RB, kx), 0) + r
            col = lax.broadcasted_iota(jnp.int32, (RB, kx), 1)
            s = jnp.where(row >= col, s, MASK_VALUE)
            e = jnp.exp(s - jnp.max(s, axis=1, keepdims=True))
            p = e / jnp.sum(e, axis=1, keepdims=True)
            PR[j, r : r + RB, :kx] = p
            c = mm(p.astype(BF16), V[:kx, :]).astype(BF16)
            C[r : r + RB, cols] = c
            CT[cols, r : r + RB] = c.T

    relay(gg)
    loads[1].wait()
    last(gg)

    def chunk_of(yt, zt):
        return (yt // 2) * (2 * NZ) + zt * 2 + yt % 2

    def a_unit(d, s, h):
        sg = 1 - 2 * d
        yt = (y - sg * (1 + s) + 2 * NY) % NY
        zt = (z - sg * (1 + h) + 2 * NZ) % NZ
        cols = pl.ds(pl.multiple_of(chunk_of(yt, zt) * CHUNK, CHUNK), CHUNK)
        rows = slice(d * A_ROWS, (d + 1) * A_ROWS)
        val = mm(CT[rows, :], G[:, cols]) * G_OUT + WO[rows, cols].astype(F32) * W_SHARE

        @pl.when(h == 0)
        def _():
            a0[d, s] = val.astype(BF16)
            remote(a0.at[d, s], ar.at[d, s, 0], a_s.at[d, s, 0], a_r.at[d, s, 0], z_dev(sg)).start()

        @pl.when(h > 0)
        def _():
            slot = ar.at[d, s, h - 1]
            remote(slot, slot, a_s.at[d, s, h - 1], a_r.at[d, s, h - 1], z_dev(sg)).wait_recv()
            total = slot[...].astype(F32) + val

            @pl.when(h < NZ - 1)
            def _():
                slot[...] = total.astype(BF16)
                remote(slot, ar.at[d, s, h], a_s.at[d, s, h], a_r.at[d, s, h], z_dev(sg)).start()

            @pl.when(h == NZ - 1)
            def _():
                @pl.when(s == 0)
                def _():
                    slot[...] = total.astype(BF16)

                @pl.when(s > 0)
                def _():
                    got = ao.at[d, s - 1]
                    remote(got, got, ao_s.at[d, s - 1], ao_r.at[d, s - 1], y_dev(sg)).wait_recv()
                    slot[...] = (total + got[...].astype(F32)).astype(BF16)

                @pl.when(s < NY - 1)
                def _():
                    remote(slot, ao.at[d, s], ao_s.at[d, s], ao_r.at[d, s], y_dev(sg)).start()

                @pl.when(s == NY - 1)
                def _():
                    sout_ref[rows, :] = slot[...]

    def b_unit(d, s, h):
        sg = 1 - 2 * d
        zt = (z - sg * (1 + s) + 2 * NZ) % NZ
        yt = (y - sg * (1 + h) + 2 * NY) % NY
        rows = pl.ds(pl.multiple_of(chunk_of(yt, zt) * CHUNK, CHUNK), CHUNK)
        cols = slice(d * B_COLS, (d + 1) * B_COLS)
        val = mm(HT[rows, :], DP[:, cols]) * G_IN + WI[rows, cols].astype(F32) * W_SHARE

        @pl.when(h == 0)
        def _():
            b0[d, s] = val.astype(BF16)
            remote(b0.at[d, s], br.at[d, s, 0], b_s.at[d, s, 0], b_r.at[d, s, 0], y_dev(sg)).start()

        @pl.when(h > 0)
        def _():
            slot = br.at[d, s, h - 1]
            remote(slot, slot, b_s.at[d, s, h - 1], b_r.at[d, s, h - 1], y_dev(sg)).wait_recv()
            total = slot[...].astype(F32) + val

            @pl.when(h < NY - 1)
            def _():
                slot[...] = total.astype(BF16)
                remote(slot, br.at[d, s, h], b_s.at[d, s, h], b_r.at[d, s, h], y_dev(sg)).start()

            @pl.when(h == NY - 1)
            def _():
                @pl.when(s == 0)
                def _():
                    slot[...] = total.astype(BF16)

                @pl.when(s > 0)
                def _():
                    got = bo.at[d, s - 1]
                    remote(got, got, bo_s.at[d, s - 1], bo_r.at[d, s - 1], z_dev(sg)).wait_recv()
                    slot[...] = (total + got[...].astype(F32)).astype(BF16)

                @pl.when(s < NZ - 1)
                def _():
                    remote(slot, bo.at[d, s], bo_s.at[d, s], bo_r.at[d, s], z_dev(sg)).start()

                @pl.when(s == NZ - 1)
                def _():
                    sin_ref[:, cols] = slot[...]

    def a_round(k):
        @pl.loop(jnp.maximum(k - (NZ - 1), 0), jnp.minimum(k, NY - 1) + 1)
        def _(s):
            a_unit(0, s, k - s)
            a_unit(1, s, k - s)

    def b_round(k):
        @pl.loop(jnp.maximum(k - (NY - 1), 0), jnp.minimum(k, NZ - 1) + 1)
        def _(s):
            b_unit(0, s, k - s)
            b_unit(1, s, k - s)

    def token_rows(xt, c):
        return pl.ds(pl.multiple_of((xt * 2 + c) * TOK, TOK), TOK)

    def sib_copy(i):
        return remote(PB.at[token_rows(i, 1 - core)], igr.at[i], sib_s.at[i], sib_r.at[i], sib)

    def x_step(h):
        for d in range(2):
            sg = 1 - 2 * d
            xt = (x - sg * (1 + h) + 2 * NX) % NX
            cols = slice(d * X_COLS, (d + 1) * X_COLS)
            term = PB[token_rows(xt, core), cols].astype(F32) + igr[xt, :, cols].astype(F32)
            if h == 0:
                x0[d] = term.astype(BF16)
                src = x0.at[d]
            else:
                src = xr.at[d, h - 1]
                remote(src, src, x_s.at[d, h - 1], x_r.at[d, h - 1], x_dev(sg)).wait_recv()
                total = (term + src[...].astype(F32)).astype(BF16)
                if h == NX - 1:
                    ig_ref[0, 0, :, cols] = total
                else:
                    src[...] = total
            if h < NX - 1:
                remote(src, xr.at[d, h], x_s.at[d, h], x_r.at[d, h], x_dev(sg)).start()

    def dcontext():
        for n in range(2):
            block = slice(n * 256, n * 256 + 256)
            DC[:, block] = (mm_nt(G[...], WO[block, :]) * SCALE_OUT).astype(BF16)
        DK[...] = jnp.zeros_like(DK)
        DV[...] = jnp.zeros_like(DV)

    def backward():
        @pl.loop(0, HEADS)
        def _(j):
            cols = pl.ds(pl.multiple_of(j * HD, HD), HD)
            for i in range(SEQ // RB):
                r, kx = i * RB, (i + 1) * RB
                dc = DC[r : r + RB, cols]
                p = PR[j, r : r + RB, :kx]
                delta = jnp.sum(
                    dc.astype(F32) * C[r : r + RB, cols].astype(F32), axis=1, keepdims=True
                )
                ds = (p * (mm_nt(dc, V[:kx, :]) - delta) * SCALE_HD).astype(BF16)
                DV[:kx, :] += mm_tn(p.astype(BF16), dc)
                DK[:kx, :] += mm_tn(ds, Q[r : r + RB, cols])
                g = mm(ds, K[:kx, :])
                cs, sn = COS[r : r + RB, :], SIN[r : r + RB, :]
                DP[r : r + RB, cols] = (g * cs + pltpu.roll(g * sn, HD // 2, 1)).astype(BF16)

        DP[:, QW : QW + HD] = unrotate(DK[...]).astype(BF16)
        DP[:, QW + HD :] = DV[...].astype(BF16)

    def input_terms():
        @pl.loop(0, D // 256)
        def _(n):
            at = pl.ds(pl.multiple_of(n * 256, 256), 256)
            PB[:, at] = (mm_nt(DP[...], WI[at, :]) * SCALE_IN).astype(BF16)

        for i in range(NX):
            sib_copy(i).start()

    LAG = 2
    ROUNDS = NY + NZ - 1

    @pl.loop(0, ROUNDS + LAG)
    def _(k):
        @pl.when(k < ROUNDS)
        def _():
            a_round(k)

        pl.when(k == 0)(dcontext)
        pl.when(k == 1)(backward)

        @pl.when(k >= LAG)
        def _():
            b_round(k - LAG)

        pl.when(k == LAG)(input_terms)

        @pl.when(k == LAG + 1)
        def _():
            for i in range(NX):
                sib_copy(i).wait_recv()
            x_step(0)

        for h in range(1, NX):
            pl.when(k == LAG + 1 + 2 * h)(functools.partial(x_step, h))

    for msgs in (gh, gg):
        for m in msgs:
            m.wait_send()
    for i in range(NX):
        sib_copy(i).wait_send()
    for d in range(2):
        for h in range(NX - 1):
            src = x0.at[d]
            remote(src, src, x_s.at[d, h], x_r.at[d, h], x_dev(1)).wait_send()

        @pl.loop(0, NY)
        def _(s):
            @pl.loop(0, NZ - 1)
            def _(h):
                src = a0.at[d, s]
                remote(src, src, a_s.at[d, s, h], a_r.at[d, s, h], z_dev(1)).wait_send()

        @pl.loop(0, NY - 1)
        def _(s):
            src = a0.at[d, s]
            remote(src, src, ao_s.at[d, s], ao_r.at[d, s], y_dev(1)).wait_send()

        @pl.loop(0, NZ)
        def _(s):
            @pl.loop(0, NY - 1)
            def _(h):
                src = b0.at[d, s]
                remote(src, src, b_s.at[d, s, h], b_r.at[d, s, h], y_dev(1)).wait_send()

        @pl.loop(0, NZ - 1)
        def _(s):
            src = b0.at[d, s]
            remote(src, src, bo_s.at[d, s], bo_r.at[d, s], z_dev(1)).wait_send()


def local(hidden_states, grad_output, w_in, w_out):
    cosine, sine = rope_tables()
    dma = pltpu.SemaphoreType.DMA
    scratch = [
        pltpu.VMEM((SEQ, D), BF16),
        pltpu.VMEM((SEQ, D), BF16),
        pltpu.VMEM((D, SEQ), BF16),
        pltpu.VMEM((D, IN_W), BF16),
        pltpu.VMEM((QW, D), BF16),
        pltpu.VMEM((SEQ, HD), F32),
        pltpu.VMEM((SEQ, HD), F32),
        pltpu.VMEM((SEQ, QW), BF16),
        pltpu.VMEM((SEQ, HD), BF16),
        pltpu.VMEM((SEQ, HD), BF16),
        pltpu.VMEM((HEADS, SEQ, SEQ), F32),
        pltpu.VMEM((SEQ, QW), BF16),
        pltpu.VMEM((QW, SEQ), BF16),
        pltpu.VMEM((SEQ, QW), BF16),
        pltpu.VMEM((SEQ, IN_W), BF16),
        pltpu.VMEM((SEQ, HD), F32),
        pltpu.VMEM((SEQ, HD), F32),
        pltpu.VMEM((2, NY, A_ROWS, CHUNK), BF16),
        pltpu.VMEM((2, NY, NZ - 1, A_ROWS, CHUNK), BF16),
        pltpu.VMEM((2, NY - 1, A_ROWS, CHUNK), BF16),
        pltpu.VMEM((2, NZ, CHUNK, B_COLS), BF16),
        pltpu.VMEM((2, NZ, NY - 1, CHUNK, B_COLS), BF16),
        pltpu.VMEM((2, NZ - 1, CHUNK, B_COLS), BF16),
        pltpu.VMEM((SEQ, D), BF16),
        pltpu.VMEM((NX, TOK, D), BF16),
        pltpu.VMEM((2, TOK, X_COLS), BF16),
        pltpu.VMEM((2, NX - 1, TOK, X_COLS), BF16),
        dma((6,)),
        dma((2, 9)), dma((2, 9)),
        dma((2, NY, NZ - 1)), dma((2, NY, NZ - 1)),
        dma((2, NY - 1)), dma((2, NY - 1)),
        dma((2, NZ, NY - 1)), dma((2, NZ, NY - 1)),
        dma((2, NZ - 1)), dma((2, NZ - 1)),
        dma((NX,)), dma((NX,)),
        dma((2, NX - 1)), dma((2, NX - 1)),
    ]
    hbm = pl.BlockSpec(memory_space=pl.ANY)
    vmem = pl.BlockSpec(memory_space=pltpu.VMEM)
    return pl.pallas_call(
        body,
        out_shape=(
            jax.ShapeDtypeStruct((1, 1, TOK, D), BF16),
            jax.ShapeDtypeStruct((CHUNK, IN_W), BF16),
            jax.ShapeDtypeStruct((QW, CHUNK), BF16),
        ),
        in_specs=[hbm] * 6,
        out_specs=(vmem, vmem, vmem),
        scratch_shapes=scratch,
        compiler_params=pltpu.CompilerParams(
            collective_id=0, has_side_effects=True, vmem_limit_bytes=60 * 1024 * 1024
        ),
        cost_estimate=pl.CostEstimate(
            flops=16_000_000_000, bytes_accessed=12_000_000, transcendentals=1_000_000
        ),
    )(hidden_states, grad_output, w_in, w_out, jnp.asarray(cosine), jnp.asarray(sine))


def solution(mesh):
    in_specs = (
        P("replica", "dp", "tensor", None),
        P("replica", "dp", "tensor", None),
        P("replica", None, "tensor"),
        P("replica", "tensor", None),
    )
    out_specs = (
        P("replica", "dp", "tensor", None),
        P(("dp", "replica"), "tensor"),
        P("tensor", ("dp", "replica")),
    )
    return jax.shard_map(local, mesh=mesh, in_specs=in_specs, out_specs=out_specs, check_vma=False)
```

```python
import functools

import jax
import jax.numpy as jnp
import numpy as np
from jax import lax
from jax.experimental import pallas as pl
from jax.experimental.pallas import tpu as pltpu
from jax.sharding import PartitionSpec as P

D = 4096
HQ = 32
HD = 128
SEQ = 512
REPLICAS = 16
NODE_DP = 2
LEARN_RATE = 0.5
ROPE_BASE = 500000.0
MASK_VALUE = -1e30

NX, NY, NZ = 4, 4, 8

HEADS = 4
QW = HEADS * HD
IN_W = QW + 2 * HD
TOK = 64
A_ROWS = QW // 4
BZ_COLS, BY_COLS = 128, 256
X_COLS = D // 2
CHUNK = D // (NY * NZ)
PAIR = 2 * CHUNK
HALF_D = D // 2
SCALE_IN = D ** (-0.5)
SCALE_OUT = (HQ * HD) ** (-0.5)
SCALE_HD = HD ** (-0.5)
W_SHARE = 1.0 / (NODE_DP * REPLICAS)
G_IN = -LEARN_RATE * SCALE_IN / REPLICAS
G_OUT = -LEARN_RATE * SCALE_OUT / REPLICAS

BF16 = jnp.bfloat16
F32 = jnp.float32


def rope_tables():
    half = HD // 2
    frequency = np.float32(ROPE_BASE) ** (
        -(np.arange(half, dtype=np.float32) * np.float32(2.0)) / np.float32(HD)
    )
    angles = np.arange(SEQ, dtype=np.float32)[:, None] * frequency[None, :].astype(np.float32)
    cosine, sine = np.cos(angles).astype(np.float32), np.sin(angles).astype(np.float32)
    return np.concatenate([cosine, cosine], 1), np.concatenate([-sine, sine], 1)


def mm(left, right):
    return lax.dot_general(left, right, (((1,), (0,)), ((), ())), preferred_element_type=F32)


def mm_nt(left, right):
    return lax.dot_general(left, right, (((1,), (1,)), ((), ())), preferred_element_type=F32)


def mm_tn(left, right):
    return lax.dot_general(left, right, (((0,), (0,)), ((), ())), preferred_element_type=F32)


def body(
    hid, gout, w_in, w_out, cos_h, sin_h,
    ig_ref, sin_ref, sout_ref,
    H, G, HT, WI, WO, TA, TB, COS, SIN, Q, K, V, PR, C, CT, DC, DA, DP, DK, DV,
    az, azo, ay, ayo, bz, bzo, by, byo, igr, x0, xr,
    lsem, ag_s, ag_r, az_s, az_r, azo_s, azo_r, ay_s, ay_r, ayo_s, ayo_r,
    bz_s, bz_r, bzo_s, bzo_r, by_s, by_r, byo_s, byo_r, sib_s, sib_r, x_s, x_r,
):
    t = lax.axis_index("tensor")
    x, core = t // 2, t % 2
    dp = lax.axis_index("dp")
    rep = lax.axis_index("replica")
    z, ylo = rep // 2, rep % 2
    y = dp * 2 + ylo

    XS, YS, ZS = {}, {}, {}
    for step in (1, -1):
        other = (y + step + NY) % NY
        XS[step] = {"tensor": ((x + step + NX) % NX) * 2 + core}
        YS[step] = {"dp": other // 2, "replica": z * 2 + other % 2}
        ZS[step] = {"replica": ((z + step + NZ) % NZ) * 2 + ylo}

    def x_dev(step):
        return XS[step]

    def y_dev(step):
        return YS[step]

    def z_dev(step):
        return ZS[step]

    sib = {"tensor": x * 2 + 1 - core}

    def remote(src, dst, ssem, rsem, dev):
        return pltpu.make_async_remote_copy(
            src_ref=src, dst_ref=dst, send_sem=ssem, recv_sem=rsem,
            device_id=dev, device_id_type=pl.DeviceIdType.MESH,
        )

    def h_rows(slot, start, size):
        return H.at[pl.ds(pl.multiple_of(slot * 2 * TOK + core * TOK + start, 32), size)]

    def g_rows(slot, start, size, cols):
        at = ((x + slot - 1 + NX) % NX) * 2 * TOK + core * TOK + start
        return G.at[pl.ds(pl.multiple_of(at, 32), size), cols]

    HALF = TOK // 2
    PLAN = (
        (None, 0, HALF, 1), (None, HALF, HALF, 1), (None, HALF, HALF, -1), (None, 0, HALF, -1), (None, 0, TOK, 0),
        (0, 0, HALF, 1), (2, HALF, HALF, -1), (0, 0, TOK, 0), (2, 0, TOK, 0), (3, 0, HALF, 0), (3, HALF, HALF, 0),
    )

    def part_z(p):
        return wrap(z + 1 + p, NZ), wrap(z - 1 - p + 4 * jnp.maximum(p - 2, 0), NZ)

    def part_cols(p):
        return [
            pl.ds(pl.multiple_of(half * HALF_D + zt * PAIR, PAIR), PAIR)
            for zt in part_z(p) for half in range(2)
        ]

    def wrap(v, n):
        below = jnp.minimum(jnp.maximum(-v, 0), 1)
        above = jnp.minimum(jnp.maximum(v - (n - 1), 0), 1)
        return v + n * below - n * above

    def upper(yt):
        return jnp.minimum(jnp.maximum(yt - 1, 0), 1)

    def copies(i, m):
        slot, start, size, step = PLAN[m]
        dev = x_dev(step) if step else sib
        here = 1 if slot is None else slot
        if i == 0:
            there = h_rows((here - step) % NX, start, size)
            src = hid.at[0, 0, pl.ds(start, size)] if slot is None else h_rows(here, start, size)
            return [remote(src, there, ag_s.at[i, m], ag_r.at[i, m], dev)]
        out = []
        for cols in part_cols(i - 1):
            there = g_rows(here, start, size, cols)
            src = gout.at[0, 0, pl.ds(start, size), cols] if slot is None else there
            out.append(remote(src, there, ag_s.at[i, m], ag_r.at[i, m], dev))
        return out

    def all_bytes(i, m):
        size = PLAN[m][2]
        ref = H.at[pl.ds(0, size)] if i == 0 else G.at[pl.ds(0, size), pl.ds(0, 4 * PAIR)]
        return remote(ref, ref, ag_s.at[i, m], ag_r.at[i, m], sib)

    def start(i, *ms):
        for m in ms:
            for copy in copies(i, m):
                copy.start()

    def got(i, *ms):
        for m in ms:
            all_bytes(i, m).wait_recv()

    def sent_all(i, *ms):
        for m in ms:
            all_bytes(i, m).wait_send()

    def direct(i):
        start(i, 0, 2, 1, 3, 4)

    def relay(i):
        for m in range(4):
            got(i, (0, 2, 1, 3)[m])
            start(i, (5, 6, 7, 8)[m])

    def share(i):
        got(i, 5)
        start(i, 9)
        got(i, 6)
        start(i, 10)

    g_own = G.at[pl.ds(pl.multiple_of((x * 2 + core) * TOK, TOK), TOK)]
    loads = [
        pltpu.make_async_copy(hid.at[0, 0], h_rows(1, 0, TOK), lsem.at[0]),
        pltpu.make_async_copy(gout.at[0, 0], g_own, lsem.at[1]),
        pltpu.make_async_copy(cos_h, COS, lsem.at[2]),
        pltpu.make_async_copy(sin_h, SIN, lsem.at[3]),
        pltpu.make_async_copy(w_in.at[0], WI, lsem.at[4]),
        pltpu.make_async_copy(w_out.at[0], WO, lsem.at[5]),
    ]
    for load in loads:
        load.start()

    barrier = pltpu.get_barrier_semaphore()
    peers = [x_dev(1), x_dev(-1), sib, y_dev(1), y_dev(-1), z_dev(1), z_dev(-1)]
    for peer in peers:
        pl.semaphore_signal(barrier, inc=1, device_id=peer, device_id_type=pl.DeviceIdType.MESH)
    pl.semaphore_wait(barrier, len(peers))

    direct(0)
    relay(0)
    direct(1)
    direct(2)
    for load in loads:
        load.wait()
    got(0, 4, 7, 8)

    def rotate(v, cosine, sine):
        return v * cosine + pltpu.roll(v, HD // 2, 1) * sine

    def unrotate(g, cosine, sine):
        return g * cosine + pltpu.roll(g * sine, HD // 2, 1)

    SHARD = 2 * TOK

    def project(slots):
        lo, hi = slots[0] * SHARD, (slots[-1] + 1) * SHARD
        at = [pl.ds(pl.multiple_of(((x + s - 1 + NX) % NX) * SHARD, SHARD), SHARD) for s in slots]
        for n in range(3):
            proj = mm(H[lo:hi, :], WI[:, n * 256 : n * 256 + 256]) * SCALE_IN
            for i, rows in enumerate(at):
                own = slice(i * SHARD, (i + 1) * SHARD)
                left, right = proj[own, :HD], proj[own, HD:]
                cosine, sine = COS[rows, :], SIN[rows, :]
                if n < 2:
                    Q[rows, n * 256 : n * 256 + HD] = rotate(left, cosine, sine).astype(BF16)
                    Q[rows, n * 256 + HD : n * 256 + 256] = rotate(right, cosine, sine).astype(BF16)
                else:
                    K[rows, :] = rotate(left, cosine, sine).astype(BF16)
                    V[rows, :] = right.astype(BF16)
        for s, rows in zip(slots, at):

            @pl.loop(0, D // 512)
            def _(n):
                c = pl.ds(pl.multiple_of(n * 512, 512), 512)
                HT[c, rows] = H[s * SHARD : (s + 1) * SHARD, c].T

    project((0, 1, 2))
    share(0)
    got(0, 9, 10)
    project((3,))
    relay(1)
    direct(3)

    RB = 128

    def forward(j):
        cols = pl.ds(pl.multiple_of(j * HD, HD), HD)
        for i in range(SEQ // RB):
            r, kx = i * RB, (i + 1) * RB
            s = mm_nt(Q[r : r + RB, cols], K[:kx, :]) * SCALE_HD
            row = lax.broadcasted_iota(jnp.int32, (RB, kx), 0) + r
            col = lax.broadcasted_iota(jnp.int32, (RB, kx), 1)
            s = jnp.where(row >= col, s, MASK_VALUE)
            e = jnp.exp(s - jnp.max(s, axis=1, keepdims=True))
            p = e * (1.0 / jnp.sum(e, axis=1, keepdims=True))
            PR[j, r : r + RB, :kx] = p
            c = mm(p.astype(BF16), V[:kx, :]).astype(BF16)
            C[r : r + RB, cols] = c
            CT[cols, r : r + RB] = c.T

    @pl.loop(0, HEADS)
    def _(j):
        forward(j)

        @pl.when(j == 1)
        def _():
            relay(2)
            direct(4)
            share(1)

    relay(3)
    share(2)

    def a_terms(p):
        for cols in part_cols(p):
            upstream = G[:, cols]
            weight = WO[:, cols]
            DA[...] += mm_nt(upstream, weight)
            grad = mm(CT[...], upstream)
            TA[:, cols] = (grad * G_OUT + weight.astype(F32) * W_SHARE).astype(BF16)

    def b_terms(p):
        for rows in part_cols(p):
            grad = mm(HT[rows, :], DP[...])
            TB[rows, :] = (grad * G_IN + WI[rows, :].astype(F32) * W_SHARE).astype(BF16)

    def hops(h, n, units):
        def first():
            for block, slots, ssems, rsems, dev, out in units:
                remote(block, slots.at[0], ssems.at[0], rsems.at[0], dev).start()

        def middle():
            for block, slots, ssems, rsems, dev, out in units:
                slot = slots.at[h - 1]
                remote(slot, slot, ssems.at[h - 1], rsems.at[h - 1], dev).wait_recv()
                slot[...] = slot[...] + block[...]
                remote(slot, slots.at[h], ssems.at[h], rsems.at[h], dev).start()

        def last():
            for block, slots, ssems, rsems, dev, out in units:
                slot = slots.at[n - 2]
                remote(slot, slot, ssems.at[n - 2], rsems.at[n - 2], dev).wait_recv()
                if out is None:
                    slot[...] = slot[...] + block[...]
                else:
                    out[...] = slot[...] + block[...]

        if isinstance(h, int):
            (first if h == 0 else last if h == n - 1 else middle)()
        else:
            pl.when(h == 0)(first)
            pl.when((h > 0) & (h < n - 1))(middle)
            pl.when(h == n - 1)(last)

    def chunk_at(yt, zt):
        at = upper(yt) * (HALF_D - PAIR) + zt * PAIR + yt * CHUNK
        return pl.ds(pl.multiple_of(at, CHUNK), CHUNK)

    def pair_at(half, zt):
        return pl.ds(pl.multiple_of(half * HALF_D + zt * PAIR, PAIR), PAIR)

    def to_y(sg, h):
        return wrap(y - sg * (1 + h), NY)

    def to_z(sg, h):
        return wrap(z - sg * (1 + h), NZ)

    def z_inside(k, piece, chunk, inner, i_s, i_r, outer, o_s, o_r, out):
        units = []
        for g in range(2):
            for d in range(2):
                sg = 1 - 2 * d
                block = piece(d, pair_at(g, to_z(sg, k)))
                units.append((block, inner.at[d, g], i_s.at[d, g], i_r.at[d, g], z_dev(sg), None))
        hops(k, NZ, units)
        j = k - (NZ - 1)

        @pl.when((j >= 0) & (j < NY))
        def _():
            units = []
            for d in range(2):
                sg = 1 - 2 * d
                yt = to_y(sg, j)
                block = chunk(inner.at[d, upper(yt), NZ - 2], yt - 2 * upper(yt))
                units.append((block, outer.at[d], o_s.at[d], o_r.at[d], y_dev(sg), out(d)))
            hops(j, NY, units)

    def y_inside(k, stages, most, piece, inner, i_s, i_r, outer, o_s, o_r, out):
        for h in reversed(range(NY)):

            @pl.when((k >= h) & (k < most + h))
            def _(h=h):
                units = []
                for s in stages(k - h):
                    for d in range(2):
                        sg = 1 - 2 * d
                        block = piece(d, chunk_at(to_y(sg, h), to_z(sg, s)))
                        units.append((block, inner.at[d, s], i_s.at[d, s], i_r.at[d, s], y_dev(sg), None))
                hops(h, NY, units)

        j = k - (NY - 1)

        @pl.when((j >= 0) & (j < NZ))
        def _():
            units = []
            for d in range(2):
                sg = 1 - 2 * d
                block = inner.at[d, j, NY - 2]
                units.append((block, outer.at[d], o_s.at[d], o_r.at[d], z_dev(sg), out(d)))
            hops(j, NZ, units)

    def lanes(ref, i):
        return ref.at[:, pl.ds(pl.multiple_of(i * CHUNK, CHUNK), CHUNK)]

    def sublanes(ref, i):
        return ref.at[pl.ds(pl.multiple_of(i * CHUNK, CHUNK), CHUNK)]

    def az_rows(d):
        return slice(d * A_ROWS, (d + 1) * A_ROWS)

    def ay_rows(d):
        return slice((2 + d) * A_ROWS, (3 + d) * A_ROWS)

    def bz_cols(d):
        return slice(d * BZ_COLS, (d + 1) * BZ_COLS)

    def by_cols(d):
        return slice(2 * BZ_COLS + d * BY_COLS, 2 * BZ_COLS + (d + 1) * BY_COLS)

    def a_round(k):
        z_inside(
            k, lambda d, at: TA.at[az_rows(d), at], lanes,
            az, az_s, az_r, azo, azo_s, azo_r, lambda d: sout_ref.at[az_rows(d)],
        )
        y_inside(
            k, lambda q: (q, 6 - q + 4 * jnp.maximum(q - 2, 0)), NZ // 2,
            lambda d, at: TA.at[ay_rows(d), at],
            ay, ay_s, ay_r, ayo, ayo_s, ayo_r, lambda d: sout_ref.at[ay_rows(d)],
        )

    def b_round(k):
        z_inside(
            k, lambda d, at: TB.at[at, bz_cols(d)], sublanes,
            bz, bz_s, bz_r, bzo, bzo_s, bzo_r, lambda d: sin_ref.at[:, bz_cols(d)],
        )
        y_inside(
            k, lambda q: (q,), NZ,
            lambda d, at: TB.at[at, by_cols(d)],
            by, by_s, by_r, byo, byo_s, byo_r, lambda d: sin_ref.at[:, by_cols(d)],
        )

    PB = H

    def token_rows(xt, c):
        return pl.ds(pl.multiple_of((xt * 2 + c) * TOK, TOK), TOK)

    def sib_copy(i):
        return remote(PB.at[token_rows(i, 1 - core)], igr.at[i], sib_s.at[i], sib_r.at[i], sib)

    def x_step(h):
        if h == 0:
            for i in range(NX):
                sib_copy(i).wait_recv()
        for d in range(2):
            sg = 1 - 2 * d
            xt = (x - sg * (1 + h) + 2 * NX) % NX
            cols = slice(d * X_COLS, (d + 1) * X_COLS)
            term = PB[token_rows(xt, core), cols].astype(F32) + igr[xt, :, cols].astype(F32)
            if h == 0:
                x0[d] = term.astype(BF16)
                src = x0.at[d]
            else:
                src = xr.at[d, h - 1]
                remote(src, src, x_s.at[d, h - 1], x_r.at[d, h - 1], x_dev(sg)).wait_recv()
                total = (term + src[...].astype(F32)).astype(BF16)
                if h == NX - 1:
                    ig_ref[0, 0, :, cols] = total
                else:
                    src[...] = total
            if h < NX - 1:
                remote(src, xr.at[d, h], x_s.at[d, h], x_r.at[d, h], x_dev(sg)).start()

    def backward(heads):
        @pl.loop(*heads)
        def _(j):
            cols = pl.ds(pl.multiple_of(j * HD, HD), HD)
            for i in range(SEQ // RB):
                r, kx = i * RB, (i + 1) * RB
                dc = DC[r : r + RB, cols]
                p = PR[j, r : r + RB, :kx]
                delta = jnp.sum(
                    dc.astype(F32) * C[r : r + RB, cols].astype(F32), axis=1, keepdims=True
                )
                ds = (p * (mm_nt(dc, V[:kx, :]) - delta) * SCALE_HD).astype(BF16)
                DV[:kx, :] += mm_tn(p.astype(BF16), dc)
                DK[:kx, :] += mm_tn(ds, Q[r : r + RB, cols])
                g = mm(ds, K[:kx, :])
                turned = unrotate(g, COS[r : r + RB, :], SIN[r : r + RB, :])
                DP[r : r + RB, cols] = turned.astype(BF16)

    def backward_first():
        DC[...] = (DA[...] * SCALE_OUT).astype(BF16)
        backward((0, 2))

    def backward_last():
        backward((2, 4))
        DP[:, QW : QW + HD] = unrotate(DK[...], COS[...], SIN[...]).astype(BF16)
        DP[:, QW + HD :] = DV[...].astype(BF16)

    def input_terms(half):
        @pl.loop(half * (D // 512), (half + 1) * (D // 512))
        def _(n):
            at = pl.ds(pl.multiple_of(n * 256, 256), 256)
            PB[:, at] = (mm_nt(DP[...], WI[at, :]) * SCALE_IN).astype(BF16)

    def input_first():
        sent_all(0, 5, 6, 7, 8, 9, 10)
        input_terms(0)

    def input_last():
        input_terms(1)
        for i in range(NX):
            sib_copy(i).start()

    DA[...] = jnp.zeros_like(DA)
    DK[...] = jnp.zeros_like(DK)
    DV[...] = jnp.zeros_like(DV)

    LAG = 5
    ROUNDS = NY + NZ - 1

    @pl.loop(0, ROUNDS + LAG)
    def _(k):
        for p in range(4):

            @pl.when(k == p)
            def _():
                got(p + 1, 4, 7, 8, 9, 10)

        @pl.when(k < 4)
        def _():
            a_terms(k)

        @pl.when(k < ROUNDS)
        def _():
            a_round(k)

        @pl.when((k >= LAG) & (k < LAG + 4))
        def _():
            b_terms(k - LAG)

        @pl.when(k >= LAG)
        def _():
            b_round(k - LAG)

        @pl.when(k == 0)
        def _():
            relay(4)
            share(3)

        pl.when(k == 1)(functools.partial(share, 4))
        pl.when(k == 3)(backward_first)
        pl.when(k == 4)(backward_last)
        pl.when(k == LAG + 1)(input_first)
        pl.when(k == LAG + 2)(input_last)
        for h in range(NX):
            pl.when(k == LAG + 3 + 2 * h)(functools.partial(x_step, h))

    sent_all(0, 0, 1, 2, 3, 4)
    for i in range(1, 5):
        sent_all(i, *range(11))
    for i in range(NX):
        sib_copy(i).wait_send()

    def sent(slots, ssems, rsems):
        @pl.loop(0, ssems.shape[0])
        def _(h):
            remote(slots.at[h], slots.at[h], ssems.at[h], rsems.at[h], sib).wait_send()

    for d in range(2):
        sent(xr.at[d], x_s.at[d], x_r.at[d])
        for outer, o_s, o_r in ((azo, azo_s, azo_r), (ayo, ayo_s, ayo_r), (bzo, bzo_s, bzo_r), (byo, byo_s, byo_r)):
            sent(outer.at[d], o_s.at[d], o_r.at[d])
        for inner, i_s, i_r in ((az, az_s, az_r), (ay, ay_s, ay_r), (bz, bz_s, bz_r), (by, by_s, by_r)):

            @pl.loop(0, i_s.shape[1])
            def _(s):
                sent(inner.at[d, s], i_s.at[d, s], i_r.at[d, s])


def finish(a_ref, b_ref, c_ref, x_ref, y_ref, w_ref):
    x_ref[...] = a_ref[...]
    y_ref[...] = b_ref[...]
    w_ref[...] = c_ref[...]


def local(hidden_states, grad_output, w_in, w_out):
    cosine, sine = rope_tables()
    dma = pltpu.SemaphoreType.DMA
    scratch = [
        pltpu.VMEM((SEQ, D), BF16),
        pltpu.VMEM((SEQ, D), BF16),
        pltpu.VMEM((D, SEQ), BF16),
        pltpu.VMEM((D, IN_W), BF16),
        pltpu.VMEM((QW, D), BF16),
        pltpu.VMEM((QW, D), BF16),
        pltpu.VMEM((D, IN_W), BF16),
        pltpu.VMEM((SEQ, HD), F32),
        pltpu.VMEM((SEQ, HD), F32),
        pltpu.VMEM((SEQ, QW), BF16),
        pltpu.VMEM((SEQ, HD), BF16),
        pltpu.VMEM((SEQ, HD), BF16),
        pltpu.VMEM((HEADS, SEQ, SEQ), F32),
        pltpu.VMEM((SEQ, QW), BF16),
        pltpu.VMEM((QW, SEQ), BF16),
        pltpu.VMEM((SEQ, QW), BF16),
        pltpu.VMEM((SEQ, QW), F32),
        pltpu.VMEM((SEQ, IN_W), BF16),
        pltpu.VMEM((SEQ, HD), F32),
        pltpu.VMEM((SEQ, HD), F32),
        pltpu.VMEM((2, 2, NZ - 1, A_ROWS, PAIR), BF16),
        pltpu.VMEM((2, NY - 1, A_ROWS, CHUNK), BF16),
        pltpu.VMEM((2, NZ, NY - 1, A_ROWS, CHUNK), BF16),
        pltpu.VMEM((2, NZ - 1, A_ROWS, CHUNK), BF16),
        pltpu.VMEM((2, 2, NZ - 1, PAIR, BZ_COLS), BF16),
        pltpu.VMEM((2, NY - 1, CHUNK, BZ_COLS), BF16),
        pltpu.VMEM((2, NZ, NY - 1, CHUNK, BY_COLS), BF16),
        pltpu.VMEM((2, NZ - 1, CHUNK, BY_COLS), BF16),
        pltpu.VMEM((NX, TOK, D), BF16),
        pltpu.VMEM((2, TOK, X_COLS), BF16),
        pltpu.VMEM((2, NX - 1, TOK, X_COLS), BF16),
        dma((6,)),
        dma((5, 11)), dma((5, 11)),
    ]
    for _ in range(2):
        scratch += [dma((2, 2, NZ - 1))] * 2 + [dma((2, NY - 1))] * 2
        scratch += [dma((2, NZ, NY - 1))] * 2 + [dma((2, NZ - 1))] * 2
    scratch += [dma((NX,))] * 2 + [dma((2, NX - 1))] * 2
    hbm = pl.BlockSpec(memory_space=pl.ANY)
    vmem = pl.BlockSpec(memory_space=pltpu.VMEM)
    shapes = (
        jax.ShapeDtypeStruct((1, 1, TOK, D), BF16),
        jax.ShapeDtypeStruct((CHUNK, IN_W), BF16),
        jax.ShapeDtypeStruct((QW, CHUNK), BF16),
    )
    outs = pl.pallas_call(
        body,
        out_shape=shapes,
        in_specs=[hbm] * 6,
        out_specs=(vmem, vmem, vmem),
        scratch_shapes=scratch,
        compiler_params=pltpu.CompilerParams(
            collective_id=0, has_side_effects=True, vmem_limit_bytes=60 * 1024 * 1024
        ),
        cost_estimate=pl.CostEstimate(
            flops=16_000_000_000, bytes_accessed=12_000_000, transcendentals=1_000_000
        ),
    )(hidden_states, grad_output, w_in, w_out, jnp.asarray(cosine), jnp.asarray(sine))
    return pl.pallas_call(
        finish,
        out_shape=shapes,
        in_specs=[vmem] * 3,
        out_specs=(vmem, vmem, vmem),
    )(*outs)


def solution(mesh):
    in_specs = (
        P("replica", "dp", "tensor", None),
        P("replica", "dp", "tensor", None),
        P("replica", None, "tensor"),
        P("replica", "tensor", None),
    )
    out_specs = (
        P("replica", "dp", "tensor", None),
        P(("dp", "replica"), "tensor"),
        P("tensor", ("dp", "replica")),
    )
    return jax.shard_map(local, mesh=mesh, in_specs=in_specs, out_specs=out_specs, check_vma=False)
```

```python
import functools

import jax
import jax.numpy as jnp
import numpy as np
from jax import lax
from jax.experimental import pallas as pl
from jax.experimental.pallas import tpu as pltpu
from jax.sharding import PartitionSpec as P

D = 4096
HQ = 32
HD = 128
SEQ = 512
REPLICAS = 16
NODE_DP = 2
LEARN_RATE = 0.5
ROPE_BASE = 500000.0
MASK_VALUE = -1e30

NX, NY, NZ = 4, 4, 8

HEADS = 4
QW = HEADS * HD
IN_W = QW + 2 * HD
TOK = 64
A_ROWS = QW // 4
BZ_COLS, BY_COLS = 128, 256
X_COLS = D // 2
CHUNK = D // (NY * NZ)
PAIR = 2 * CHUNK
HALF_D = D // 2
SCALE_IN = D ** (-0.5)
SCALE_OUT = (HQ * HD) ** (-0.5)
SCALE_HD = HD ** (-0.5)
W_SHARE = 1.0 / (NODE_DP * REPLICAS)
G_IN = -LEARN_RATE * SCALE_IN / REPLICAS
G_OUT = -LEARN_RATE * SCALE_OUT / REPLICAS

BF16 = jnp.bfloat16
F32 = jnp.float32


def rope_tables():
    half = HD // 2
    frequency = np.float32(ROPE_BASE) ** (
        -(np.arange(half, dtype=np.float32) * np.float32(2.0)) / np.float32(HD)
    )
    angles = np.arange(SEQ, dtype=np.float32)[:, None] * frequency[None, :].astype(np.float32)
    cosine, sine = np.cos(angles).astype(np.float32), np.sin(angles).astype(np.float32)
    return np.concatenate([cosine, cosine], 1), np.concatenate([-sine, sine], 1)


def mm(left, right):
    return lax.dot_general(left, right, (((1,), (0,)), ((), ())), preferred_element_type=F32)


def mm_nt(left, right):
    return lax.dot_general(left, right, (((1,), (1,)), ((), ())), preferred_element_type=F32)


def mm_tn(left, right):
    return lax.dot_general(left, right, (((0,), (0,)), ((), ())), preferred_element_type=F32)


def body(
    hid, gout, w_in, w_out, cos_h, sin_h,
    ig_ref, sin_ref, sout_ref,
    H, G, HT, WI, WO, TA, TB, COS, SIN, Q, K, V, PR, C, CT, DC, DA, DP, DK, DV,
    az, azo, ay, ayo, bz, bzo, by, byo, igr, x0, xr,
    lsem, ag_s, ag_r, az_s, az_r, azo_s, azo_r, ay_s, ay_r, ayo_s, ayo_r,
    bz_s, bz_r, bzo_s, bzo_r, by_s, by_r, byo_s, byo_r, sib_s, sib_r, x_s, x_r,
):
    t = lax.axis_index("tensor")
    x, core = t // 2, t % 2
    dp = lax.axis_index("dp")
    rep = lax.axis_index("replica")
    z, ylo = rep // 2, rep % 2
    y = dp * 2 + ylo

    XS, YS, ZS = {}, {}, {}
    for step in (1, -1):
        other = (y + step + NY) % NY
        XS[step] = {"tensor": ((x + step + NX) % NX) * 2 + core}
        YS[step] = {"dp": other // 2, "replica": z * 2 + other % 2}
        ZS[step] = {"replica": ((z + step + NZ) % NZ) * 2 + ylo}

    def x_dev(step):
        return XS[step]

    def y_dev(step):
        return YS[step]

    def z_dev(step):
        return ZS[step]

    sib = {"tensor": x * 2 + 1 - core}

    def remote(src, dst, ssem, rsem, dev):
        return pltpu.make_async_remote_copy(
            src_ref=src, dst_ref=dst, send_sem=ssem, recv_sem=rsem,
            device_id=dev, device_id_type=pl.DeviceIdType.MESH,
        )

    def h_rows(slot, start, size):
        return H.at[pl.ds(pl.multiple_of(slot * 2 * TOK + core * TOK + start, 32), size)]

    def g_rows(slot, start, size, cols):
        at = ((x + slot - 1 + NX) % NX) * 2 * TOK + core * TOK + start
        return G.at[pl.ds(pl.multiple_of(at, 32), size), cols]

    HALF = TOK // 2
    PLAN = (
        (None, 0, HALF, 1), (None, HALF, HALF, 1), (None, HALF, HALF, -1), (None, 0, HALF, -1), (None, 0, TOK, 0),
        (0, 0, HALF, 1), (2, HALF, HALF, -1), (0, 0, TOK, 0), (2, 0, TOK, 0), (3, 0, HALF, 0), (3, HALF, HALF, 0),
    )

    def part_z(p):
        return wrap(z - NZ // 2 + p, NZ), wrap(z + NZ // 2 - 1 - p, NZ)

    def part_cols(p):
        return [
            pl.ds(pl.multiple_of(half * HALF_D + zt * PAIR, PAIR), PAIR)
            for zt in part_z(p) for half in range(2)
        ]

    def wrap(v, n):
        below = jnp.minimum(jnp.maximum(-v, 0), 1)
        above = jnp.minimum(jnp.maximum(v - (n - 1), 0), 1)
        return v + n * below - n * above

    def upper(yt):
        return jnp.minimum(jnp.maximum(yt - 1, 0), 1)

    def copies(i, m):
        slot, start, size, step = PLAN[m]
        dev = x_dev(step) if step else sib
        here = 1 if slot is None else slot
        if i == 0:
            there = h_rows((here - step) % NX, start, size)
            src = hid.at[0, 0, pl.ds(start, size)] if slot is None else h_rows(here, start, size)
            return [remote(src, there, ag_s.at[i, m], ag_r.at[i, m], dev)]
        out = []
        for cols in part_cols(i - 1):
            there = g_rows(here, start, size, cols)
            src = gout.at[0, 0, pl.ds(start, size), cols] if slot is None else there
            out.append(remote(src, there, ag_s.at[i, m], ag_r.at[i, m], dev))
        return out

    def all_bytes(i, m):
        size = PLAN[m][2]
        ref = H.at[pl.ds(0, size)] if i == 0 else G.at[pl.ds(0, size), pl.ds(0, 4 * PAIR)]
        return remote(ref, ref, ag_s.at[i, m], ag_r.at[i, m], sib)

    def start(i, *ms):
        for m in ms:
            for copy in copies(i, m):
                copy.start()

    def got(i, *ms):
        for m in ms:
            all_bytes(i, m).wait_recv()

    def sent_all(i, *ms):
        for m in ms:
            all_bytes(i, m).wait_send()

    def direct(i):
        start(i, 0, 2, 1, 3, 4)

    def relay(i):
        for m in range(4):
            got(i, (0, 2, 1, 3)[m])
            start(i, (5, 6, 7, 8)[m])

    def share(i):
        got(i, 5)
        start(i, 9)
        got(i, 6)
        start(i, 10)

    g_own = G.at[pl.ds(pl.multiple_of((x * 2 + core) * TOK, TOK), TOK)]
    loads = [
        pltpu.make_async_copy(hid.at[0, 0], h_rows(1, 0, TOK), lsem.at[0]),
        pltpu.make_async_copy(gout.at[0, 0], g_own, lsem.at[1]),
        pltpu.make_async_copy(cos_h, COS, lsem.at[2]),
        pltpu.make_async_copy(sin_h, SIN, lsem.at[3]),
        pltpu.make_async_copy(w_in.at[0], WI, lsem.at[4]),
        pltpu.make_async_copy(w_out.at[0], WO, lsem.at[5]),
    ]
    for load in loads:
        load.start()

    barrier = pltpu.get_barrier_semaphore()
    peers = [x_dev(1), x_dev(-1), sib, y_dev(1), y_dev(-1), z_dev(1), z_dev(-1)]
    for peer in peers:
        pl.semaphore_signal(barrier, inc=1, device_id=peer, device_id_type=pl.DeviceIdType.MESH)
    pl.semaphore_wait(barrier, len(peers))

    direct(0)
    relay(0)
    direct(1)
    direct(2)
    for load in loads:
        load.wait()
    got(0, 4, 7, 8)

    def rotate(v, cosine, sine):
        return v * cosine + pltpu.roll(v, HD // 2, 1) * sine

    def unrotate(g, cosine, sine):
        return g * cosine + pltpu.roll(g * sine, HD // 2, 1)

    SHARD = 2 * TOK

    def project(slots):
        lo, hi = slots[0] * SHARD, (slots[-1] + 1) * SHARD
        at = [pl.ds(pl.multiple_of(((x + s - 1 + NX) % NX) * SHARD, SHARD), SHARD) for s in slots]
        for n in range(3):
            proj = mm(H[lo:hi, :], WI[:, n * 256 : n * 256 + 256]) * SCALE_IN
            for i, rows in enumerate(at):
                own = slice(i * SHARD, (i + 1) * SHARD)
                left, right = proj[own, :HD], proj[own, HD:]
                cosine, sine = COS[rows, :], SIN[rows, :]
                if n < 2:
                    Q[rows, n * 256 : n * 256 + HD] = rotate(left, cosine, sine).astype(BF16)
                    Q[rows, n * 256 + HD : n * 256 + 256] = rotate(right, cosine, sine).astype(BF16)
                else:
                    K[rows, :] = rotate(left, cosine, sine).astype(BF16)
                    V[rows, :] = right.astype(BF16)
        for s, rows in zip(slots, at):

            @pl.loop(0, D // 512)
            def _(n):
                c = pl.ds(pl.multiple_of(n * 512, 512), 512)
                HT[c, rows] = H[s * SHARD : (s + 1) * SHARD, c].T

    project((0, 1, 2))
    share(0)
    got(0, 9, 10)
    project((3,))
    relay(1)
    direct(3)

    RB = 128

    def forward(j):
        cols = pl.ds(pl.multiple_of(j * HD, HD), HD)
        for i in range(SEQ // RB):
            r, kx = i * RB, (i + 1) * RB
            s = mm_nt(Q[r : r + RB, cols], K[:kx, :]) * SCALE_HD
            row = lax.broadcasted_iota(jnp.int32, (RB, kx), 0) + r
            col = lax.broadcasted_iota(jnp.int32, (RB, kx), 1)
            s = jnp.where(row >= col, s, MASK_VALUE)
            e = jnp.exp(s - jnp.max(s, axis=1, keepdims=True))
            p = e * (1.0 / jnp.sum(e, axis=1, keepdims=True))
            PR[j, r : r + RB, :kx] = p
            c = mm(p.astype(BF16), V[:kx, :]).astype(BF16)
            C[r : r + RB, cols] = c
            CT[cols, r : r + RB] = c.T

    @pl.loop(0, HEADS)
    def _(j):
        forward(j)

        @pl.when(j == 1)
        def _():
            relay(2)
            direct(4)
            share(1)

    relay(3)
    share(2)

    def a_terms(p):
        for cols in part_cols(p):
            upstream = G[:, cols]
            weight = WO[:, cols]
            DA[...] += mm_nt(upstream, weight)
            grad = mm(CT[...], upstream)
            TA[:, cols] = (grad * G_OUT + weight.astype(F32) * W_SHARE).astype(BF16)

    def b_terms(p):
        for rows in part_cols(p):
            grad = mm(HT[rows, :], DP[...])
            TB[rows, :] = (grad * G_IN + WI[rows, :].astype(F32) * W_SHARE).astype(BF16)

    def length(n, e, sg):
        return n // 2 - (0 if (e == 0) == (sg == 1) else 1)

    def step(dist, n, e, sg, block, slots, ssems, rsems, dev):
        if dist > length(n, e, sg):
            return
        h = length(n, e, sg) - dist
        i = h + (0 if sg == 1 else length(n, e, 1))
        src = block
        if h > 0:
            src = slots.at[i - 1]
            remote(src, src, ssems.at[i - 1], rsems.at[i - 1], dev).wait_recv()
            src[...] = src[...] + block[...]
        remote(src, slots.at[i], ssems.at[i], rsems.at[i], dev).start()

    def total_at(n, e):
        return length(n, e, 1) - 1

    def last(n, e, block, slots, ssems, rsems, out=None):
        terms = [block[...].astype(F32)]
        for i in (total_at(n, e), n - 2):
            slot = slots.at[i]
            remote(slot, slot, ssems.at[i], rsems.at[i], sib).wait_recv()
            terms.append(slot[...].astype(F32))
        out = slots.at[total_at(n, e)] if out is None else out
        out[...] = (terms[0] + terms[1] + terms[2]).astype(BF16)

    def chunk_at(yt, zt):
        at = upper(yt) * (HALF_D - PAIR) + zt * PAIR + yt * CHUNK
        return pl.ds(pl.multiple_of(at, CHUNK), CHUNK)

    def pair_at(half, zt):
        return pl.ds(pl.multiple_of(half * HALF_D + zt * PAIR, PAIR), PAIR)

    WAYS = [(e, sg) for e in range(2) for sg in (1, -1)]

    def z_inside(k, piece, chunk, inner, i_s, i_r, outer, o_s, o_r, out):
        half = NZ // 2

        def inside(g):
            for i in range(half):

                @pl.when(k == i)
                def _(dist=half - i):
                    for e, sg in WAYS:
                        block = piece(e, pair_at(g, wrap(z + sg * dist, NZ)))
                        step(dist, NZ, e, sg, block, inner.at[e, g], i_s.at[e, g], i_r.at[e, g], z_dev(sg))

            @pl.when(k == half)
            def _():
                for e in range(2):
                    last(NZ, e, piece(e, pair_at(g, z)), inner.at[e, g], i_s.at[e, g], i_r.at[e, g])

        def chunk_of(e, yt):
            return chunk(inner.at[e, upper(yt), total_at(NZ, e)], yt - 2 * upper(yt))

        def outside():
            for dist in (2, 1):

                @pl.when(k == half + 2 - dist)
                def _(dist=dist):
                    for e, sg in WAYS:
                        block = chunk_of(e, wrap(y + sg * dist, NY))
                        step(dist, NY, e, sg, block, outer.at[e], o_s.at[e], o_r.at[e], y_dev(sg))

            @pl.when(k == half + 2)
            def _():
                for e in range(2):
                    last(NY, e, chunk_of(e, y), outer.at[e], o_s.at[e], o_r.at[e], out(e))

        return inside, outside

    def y_inside(k, piece, inner, i_s, i_r, outer, o_s, o_r, out):
        half = NZ // 2

        def one(dist, s, zt):
            for e, sg in WAYS:
                if dist > 0:
                    block = piece(e, chunk_at(wrap(y + sg * dist, NY), zt))
                    step(dist, NY, e, sg, block, inner.at[e, s], i_s.at[e, s], i_r.at[e, s], y_dev(sg))
                elif sg == 1:
                    last(NY, e, piece(e, chunk_at(y, zt)), inner.at[e, s], i_s.at[e, s], i_r.at[e, s])

        def inside(dist):
            g = k - (2 - dist)

            @pl.when((g >= 0) & (g <= half))
            def _():
                one(dist, half - g, wrap(z + half - g, NZ))

            @pl.when((g > 0) & (g < half))
            def _():
                one(dist, half + g, wrap(z - half + g, NZ))

        def outside():
            for dist in range(half, 0, -1):

                @pl.when(k == half + 2 - dist)
                def _(dist=dist):
                    for e, sg in WAYS:
                        block = inner.at[e, dist if sg == 1 else NZ - dist, total_at(NY, e)]
                        step(dist, NZ, e, sg, block, outer.at[e], o_s.at[e], o_r.at[e], z_dev(sg))

            @pl.when(k == half + 2)
            def _():
                for e in range(2):
                    block = inner.at[e, 0, total_at(NY, e)]
                    last(NZ, e, block, outer.at[e], o_s.at[e], o_r.at[e], out(e))

        return inside, outside

    def both(z_part, y_part):
        z_in, z_out = z_part
        y_in, y_out = y_part
        y_in(2)
        z_in(0)
        y_in(1)
        z_in(1)
        y_in(0)
        y_out()
        z_out()

    def lanes(ref, i):
        return ref.at[:, pl.ds(pl.multiple_of(i * CHUNK, CHUNK), CHUNK)]

    def sublanes(ref, i):
        return ref.at[pl.ds(pl.multiple_of(i * CHUNK, CHUNK), CHUNK)]

    def az_rows(d):
        return slice(d * A_ROWS, (d + 1) * A_ROWS)

    def ay_rows(d):
        return slice((2 + d) * A_ROWS, (3 + d) * A_ROWS)

    def bz_cols(d):
        return slice(d * BZ_COLS, (d + 1) * BZ_COLS)

    def by_cols(d):
        return slice(2 * BZ_COLS + d * BY_COLS, 2 * BZ_COLS + (d + 1) * BY_COLS)

    def a_round(k):
        z_part = z_inside(
            k, lambda d, at: TA.at[az_rows(d), at], lanes,
            az, az_s, az_r, azo, azo_s, azo_r, lambda d: sout_ref.at[az_rows(d)],
        )
        y_part = y_inside(
            k, lambda d, at: TA.at[ay_rows(d), at],
            ay, ay_s, ay_r, ayo, ayo_s, ayo_r, lambda d: sout_ref.at[ay_rows(d)],
        )
        both(z_part, y_part)

    def b_round(k):
        z_part = z_inside(
            k, lambda d, at: TB.at[at, bz_cols(d)], sublanes,
            bz, bz_s, bz_r, bzo, bzo_s, bzo_r, lambda d: sin_ref.at[:, bz_cols(d)],
        )
        y_part = y_inside(
            k, lambda d, at: TB.at[at, by_cols(d)],
            by, by_s, by_r, byo, byo_s, byo_r, lambda d: sin_ref.at[:, by_cols(d)],
        )
        both(z_part, y_part)

    PB = H

    def token_rows(xt, c):
        return pl.ds(pl.multiple_of((xt * 2 + c) * TOK, TOK), TOK)

    def sib_copy(i):
        return remote(PB.at[token_rows(i, 1 - core)], igr.at[i], sib_s.at[i], sib_r.at[i], sib)

    def x_step(h):
        if h == 0:
            for i in range(NX):
                sib_copy(i).wait_recv()
        for d in range(2):
            sg = 1 - 2 * d
            xt = (x - sg * (1 + h) + 2 * NX) % NX
            cols = slice(d * X_COLS, (d + 1) * X_COLS)
            term = PB[token_rows(xt, core), cols].astype(F32) + igr[xt, :, cols].astype(F32)
            if h == 0:
                x0[d] = term.astype(BF16)
                src = x0.at[d]
            else:
                src = xr.at[d, h - 1]
                remote(src, src, x_s.at[d, h - 1], x_r.at[d, h - 1], x_dev(sg)).wait_recv()
                total = (term + src[...].astype(F32)).astype(BF16)
                if h == NX - 1:
                    ig_ref[0, 0, :, cols] = total
                else:
                    src[...] = total
            if h < NX - 1:
                remote(src, xr.at[d, h], x_s.at[d, h], x_r.at[d, h], x_dev(sg)).start()

    def backward(heads):
        @pl.loop(*heads)
        def _(j):
            cols = pl.ds(pl.multiple_of(j * HD, HD), HD)
            for i in range(SEQ // RB):
                r, kx = i * RB, (i + 1) * RB
                dc = DC[r : r + RB, cols]
                p = PR[j, r : r + RB, :kx]
                delta = jnp.sum(
                    dc.astype(F32) * C[r : r + RB, cols].astype(F32), axis=1, keepdims=True
                )
                ds = (p * (mm_nt(dc, V[:kx, :]) - delta) * SCALE_HD).astype(BF16)
                DV[:kx, :] += mm_tn(p.astype(BF16), dc)
                DK[:kx, :] += mm_tn(ds, Q[r : r + RB, cols])
                g = mm(ds, K[:kx, :])
                turned = unrotate(g, COS[r : r + RB, :], SIN[r : r + RB, :])
                DP[r : r + RB, cols] = turned.astype(BF16)

    def backward_first():
        DC[...] = (DA[...] * SCALE_OUT).astype(BF16)
        backward((0, 2))

    def backward_last():
        backward((2, 4))
        DP[:, QW : QW + HD] = unrotate(DK[...], COS[...], SIN[...]).astype(BF16)
        DP[:, QW + HD :] = DV[...].astype(BF16)

    def input_terms(half):
        @pl.loop(half * (D // 512), (half + 1) * (D // 512))
        def _(n):
            at = pl.ds(pl.multiple_of(n * 256, 256), 256)
            PB[:, at] = (mm_nt(DP[...], WI[at, :]) * SCALE_IN).astype(BF16)

    def input_first():
        sent_all(0, 5, 6, 7, 8, 9, 10)
        input_terms(0)

    def input_last():
        input_terms(1)
        for i in range(NX):
            sib_copy(i).start()

    DA[...] = jnp.zeros_like(DA)
    DK[...] = jnp.zeros_like(DK)
    DV[...] = jnp.zeros_like(DV)

    LAG = 5
    ROUNDS = NY // 2 + NZ // 2 + 1

    got(1, 4, 7, 8, 9, 10)
    a_terms(0)

    @pl.loop(0, ROUNDS + LAG)
    def _(k):
        @pl.when(k < ROUNDS)
        def _():
            a_round(k)

        @pl.when(k >= LAG)
        def _():
            b_round(k - LAG)

        pl.when(k == 0)(functools.partial(share, 3))
        for p in range(1, 4):

            @pl.when(k == p - 1)
            def _(p=p):
                got(p + 1, 4, 7, 8, 9, 10)

        @pl.when(k < 3)
        def _():
            a_terms(k + 1)

        pl.when(k == 0)(functools.partial(relay, 4))
        pl.when(k == 1)(functools.partial(share, 4))
        pl.when(k == 3)(backward_first)
        pl.when(k == 4)(backward_last)

        @pl.when((k >= LAG - 1) & (k < LAG + 3))
        def _():
            b_terms(k - LAG + 1)

        pl.when(k == LAG)(input_first)
        pl.when(k == LAG + 1)(input_last)
        for h, at in enumerate((2, 3, 4, 6)):
            pl.when(k == LAG + at)(functools.partial(x_step, h))

    sent_all(0, 0, 1, 2, 3, 4)
    for i in range(1, 5):
        sent_all(i, *range(11))
    for i in range(NX):
        sib_copy(i).wait_send()

    def sent(slots, ssems, rsems):
        @pl.loop(0, ssems.shape[0])
        def _(h):
            remote(slots.at[h], slots.at[h], ssems.at[h], rsems.at[h], sib).wait_send()

    for d in range(2):
        sent(xr.at[d], x_s.at[d], x_r.at[d])
        for outer, o_s, o_r in ((azo, azo_s, azo_r), (ayo, ayo_s, ayo_r), (bzo, bzo_s, bzo_r), (byo, byo_s, byo_r)):
            sent(outer.at[d], o_s.at[d], o_r.at[d])
        for inner, i_s, i_r in ((az, az_s, az_r), (ay, ay_s, ay_r), (bz, bz_s, bz_r), (by, by_s, by_r)):

            @pl.loop(0, i_s.shape[1])
            def _(s):
                sent(inner.at[d, s], i_s.at[d, s], i_r.at[d, s])


def finish(a_ref, b_ref, c_ref, x_ref, y_ref, w_ref):
    x_ref[...] = a_ref[...]
    y_ref[...] = b_ref[...]
    w_ref[...] = c_ref[...]


def local(hidden_states, grad_output, w_in, w_out):
    cosine, sine = rope_tables()
    dma = pltpu.SemaphoreType.DMA
    scratch = [
        pltpu.VMEM((SEQ, D), BF16),
        pltpu.VMEM((SEQ, D), BF16),
        pltpu.VMEM((D, SEQ), BF16),
        pltpu.VMEM((D, IN_W), BF16),
        pltpu.VMEM((QW, D), BF16),
        pltpu.VMEM((QW, D), BF16),
        pltpu.VMEM((D, IN_W), BF16),
        pltpu.VMEM((SEQ, HD), F32),
        pltpu.VMEM((SEQ, HD), F32),
        pltpu.VMEM((SEQ, QW), BF16),
        pltpu.VMEM((SEQ, HD), BF16),
        pltpu.VMEM((SEQ, HD), BF16),
        pltpu.VMEM((HEADS, SEQ, SEQ), F32),
        pltpu.VMEM((SEQ, QW), BF16),
        pltpu.VMEM((QW, SEQ), BF16),
        pltpu.VMEM((SEQ, QW), BF16),
        pltpu.VMEM((SEQ, QW), F32),
        pltpu.VMEM((SEQ, IN_W), BF16),
        pltpu.VMEM((SEQ, HD), F32),
        pltpu.VMEM((SEQ, HD), F32),
        pltpu.VMEM((2, 2, NZ - 1, A_ROWS, PAIR), BF16),
        pltpu.VMEM((2, NY - 1, A_ROWS, CHUNK), BF16),
        pltpu.VMEM((2, NZ, NY - 1, A_ROWS, CHUNK), BF16),
        pltpu.VMEM((2, NZ - 1, A_ROWS, CHUNK), BF16),
        pltpu.VMEM((2, 2, NZ - 1, PAIR, BZ_COLS), BF16),
        pltpu.VMEM((2, NY - 1, CHUNK, BZ_COLS), BF16),
        pltpu.VMEM((2, NZ, NY - 1, CHUNK, BY_COLS), BF16),
        pltpu.VMEM((2, NZ - 1, CHUNK, BY_COLS), BF16),
        pltpu.VMEM((NX, TOK, D), BF16),
        pltpu.VMEM((2, TOK, X_COLS), BF16),
        pltpu.VMEM((2, NX - 1, TOK, X_COLS), BF16),
        dma((6,)),
        dma((5, 11)), dma((5, 11)),
    ]
    for _ in range(2):
        scratch += [dma((2, 2, NZ - 1))] * 2 + [dma((2, NY - 1))] * 2
        scratch += [dma((2, NZ, NY - 1))] * 2 + [dma((2, NZ - 1))] * 2
    scratch += [dma((NX,))] * 2 + [dma((2, NX - 1))] * 2
    hbm = pl.BlockSpec(memory_space=pl.ANY)
    vmem = pl.BlockSpec(memory_space=pltpu.VMEM)
    shapes = (
        jax.ShapeDtypeStruct((1, 1, TOK, D), BF16),
        jax.ShapeDtypeStruct((CHUNK, IN_W), BF16),
        jax.ShapeDtypeStruct((QW, CHUNK), BF16),
    )
    outs = pl.pallas_call(
        body,
        out_shape=shapes,
        in_specs=[hbm] * 6,
        out_specs=(vmem, vmem, vmem),
        scratch_shapes=scratch,
        compiler_params=pltpu.CompilerParams(
            collective_id=0, has_side_effects=True, vmem_limit_bytes=60 * 1024 * 1024
        ),
        cost_estimate=pl.CostEstimate(
            flops=16_000_000_000, bytes_accessed=12_000_000, transcendentals=1_000_000
        ),
    )(hidden_states, grad_output, w_in, w_out, jnp.asarray(cosine), jnp.asarray(sine))
    return pl.pallas_call(
        finish,
        out_shape=shapes,
        in_specs=[vmem] * 3,
        out_specs=(vmem, vmem, vmem),
    )(*outs)


def solution(mesh):
    in_specs = (
        P("replica", "dp", "tensor", None),
        P("replica", "dp", "tensor", None),
        P("replica", None, "tensor"),
        P("replica", "tensor", None),
    )
    out_specs = (
        P("replica", "dp", "tensor", None),
        P(("dp", "replica"), "tensor"),
        P("tensor", ("dp", "replica")),
    )
    return jax.shard_map(local, mesh=mesh, in_specs=in_specs, out_specs=out_specs, check_vma=False)
```

```python
import functools

import jax
import jax.numpy as jnp
import numpy as np
from jax import lax
from jax.experimental import pallas as pl
from jax.experimental.pallas import tpu as pltpu
from jax.sharding import PartitionSpec as P

D = 4096
HQ = 32
HD = 128
SEQ = 512
REPLICAS = 16
NODE_DP = 2
LEARN_RATE = 0.5
ROPE_BASE = 500000.0
MASK_VALUE = -1e30

NX, NY, NZ = 4, 4, 8

HEADS = 4
QW = HEADS * HD
IN_W = QW + 2 * HD
TOK = 64
A_ROWS = QW // 4
BZ_COLS, BY_COLS = 128, 256
X_COLS = D // 2
CHUNK = D // (NY * NZ)
PAIR = 2 * CHUNK
HALF_D = D // 2
SCALE_IN = D ** (-0.5)
SCALE_OUT = (HQ * HD) ** (-0.5)
SCALE_HD = HD ** (-0.5)
W_SHARE = 1.0 / (NODE_DP * REPLICAS)
G_IN = -LEARN_RATE * SCALE_IN / REPLICAS
G_OUT = -LEARN_RATE * SCALE_OUT / REPLICAS

BF16 = jnp.bfloat16
F32 = jnp.float32


def rope_tables():
    half = HD // 2
    frequency = np.float32(ROPE_BASE) ** (
        -(np.arange(half, dtype=np.float32) * np.float32(2.0)) / np.float32(HD)
    )
    angles = np.arange(SEQ, dtype=np.float32)[:, None] * frequency[None, :].astype(np.float32)
    cosine, sine = np.cos(angles).astype(np.float32), np.sin(angles).astype(np.float32)
    return np.concatenate([cosine, cosine], 1), np.concatenate([-sine, sine], 1)


def mm(left, right):
    return lax.dot_general(left, right, (((1,), (0,)), ((), ())), preferred_element_type=F32)


def mm_nt(left, right):
    return lax.dot_general(left, right, (((1,), (1,)), ((), ())), preferred_element_type=F32)


def mm_tn(left, right):
    return lax.dot_general(left, right, (((0,), (0,)), ((), ())), preferred_element_type=F32)


def body(
    hid, gout, w_in, w_out, cos_h, sin_h,
    ig_ref, sin_ref, sout_ref,
    H, G, HT, WI, WO, TA, TB, COS, SIN, Q, K, V, PR, C, CT, DC, DA, DP, DK, DV,
    az, azo, ay, ayo, bz, bzo, by, byo, igr, x0, xr,
    lsem, ag_s, ag_r, az_s, az_r, azo_s, azo_r, ay_s, ay_r, ayo_s, ayo_r,
    bz_s, bz_r, bzo_s, bzo_r, by_s, by_r, byo_s, byo_r, sib_s, sib_r, x_s, x_r,
):
    t = lax.axis_index("tensor")
    x, core = t // 2, t % 2
    dp = lax.axis_index("dp")
    rep = lax.axis_index("replica")
    z, ylo = rep // 2, rep % 2
    y = dp * 2 + ylo

    XS, YS, ZS = {}, {}, {}
    for step in (1, -1):
        other = (y + step + NY) % NY
        XS[step] = {"tensor": ((x + step + NX) % NX) * 2 + core}
        YS[step] = {"dp": other // 2, "replica": z * 2 + other % 2}
        ZS[step] = {"replica": ((z + step + NZ) % NZ) * 2 + ylo}

    def x_dev(step):
        return XS[step]

    def y_dev(step):
        return YS[step]

    def z_dev(step):
        return ZS[step]

    sib = {"tensor": x * 2 + 1 - core}

    def remote(src, dst, ssem, rsem, dev):
        return pltpu.make_async_remote_copy(
            src_ref=src, dst_ref=dst, send_sem=ssem, recv_sem=rsem,
            device_id=dev, device_id_type=pl.DeviceIdType.MESH,
        )

    def h_rows(slot, start, size):
        return H.at[pl.ds(pl.multiple_of(slot * 2 * TOK + core * TOK + start, 32), size)]

    def g_rows(slot, start, size, cols):
        at = ((x + slot - 1 + NX) % NX) * 2 * TOK + core * TOK + start
        return G.at[pl.ds(pl.multiple_of(at, 32), size), cols]

    HALF = TOK // 2
    PLAN = (
        (None, 0, HALF, 1), (None, HALF, HALF, 1), (None, HALF, HALF, -1), (None, 0, HALF, -1), (None, 0, TOK, 0),
        (0, 0, HALF, 1), (2, HALF, HALF, -1), (0, 0, TOK, 0), (2, 0, TOK, 0), (3, 0, HALF, 0), (3, HALF, HALF, 0),
    )

    def part_z(p):
        return wrap(z - NZ // 2 + p, NZ), wrap(z + NZ // 2 - 1 - p, NZ)

    def part_cols(p):
        return [
            pl.ds(pl.multiple_of(half * HALF_D + zt * PAIR, PAIR), PAIR)
            for zt in part_z(p) for half in range(2)
        ]

    def wrap(v, n):
        below = jnp.minimum(jnp.maximum(-v, 0), 1)
        above = jnp.minimum(jnp.maximum(v - (n - 1), 0), 1)
        return v + n * below - n * above

    def upper(yt):
        return jnp.minimum(jnp.maximum(yt - 1, 0), 1)

    def copies(i, m):
        slot, start, size, step = PLAN[m]
        dev = x_dev(step) if step else sib
        here = 1 if slot is None else slot
        if i == 0:
            there = h_rows((here - step) % NX, start, size)
            src = hid.at[0, 0, pl.ds(start, size)] if slot is None else h_rows(here, start, size)
            return [remote(src, there, ag_s.at[i, m], ag_r.at[i, m], dev)]
        out = []
        for cols in part_cols(i - 1):
            there = g_rows(here, start, size, cols)
            src = gout.at[0, 0, pl.ds(start, size), cols] if slot is None else there
            out.append(remote(src, there, ag_s.at[i, m], ag_r.at[i, m], dev))
        return out

    def all_bytes(i, m):
        size = PLAN[m][2]
        ref = H.at[pl.ds(0, size)] if i == 0 else G.at[pl.ds(0, size), pl.ds(0, 4 * PAIR)]
        return remote(ref, ref, ag_s.at[i, m], ag_r.at[i, m], sib)

    def start(i, *ms):
        for m in ms:
            for copy in copies(i, m):
                copy.start()

    def got(i, *ms):
        for m in ms:
            all_bytes(i, m).wait_recv()

    def sent_all(i, *ms):
        for m in ms:
            all_bytes(i, m).wait_send()

    def direct(i):
        start(i, 0, 2, 1, 3, 4)

    def relay(i):
        for m in range(4):
            got(i, (0, 2, 1, 3)[m])
            start(i, (5, 6, 7, 8)[m])

    def share(i):
        got(i, 5)
        start(i, 9)
        got(i, 6)
        start(i, 10)

    g_own = G.at[pl.ds(pl.multiple_of((x * 2 + core) * TOK, TOK), TOK)]
    loads = [
        pltpu.make_async_copy(hid.at[0, 0], h_rows(1, 0, TOK), lsem.at[0]),
        pltpu.make_async_copy(gout.at[0, 0], g_own, lsem.at[1]),
        pltpu.make_async_copy(cos_h, COS, lsem.at[2]),
        pltpu.make_async_copy(sin_h, SIN, lsem.at[3]),
        pltpu.make_async_copy(w_in.at[0], WI, lsem.at[4]),
        pltpu.make_async_copy(w_out.at[0], WO, lsem.at[5]),
    ]
    for load in loads:
        load.start()

    barrier = pltpu.get_barrier_semaphore()
    peers = [x_dev(1), x_dev(-1), sib, y_dev(1), y_dev(-1), z_dev(1), z_dev(-1)]
    for peer in peers:
        pl.semaphore_signal(barrier, inc=1, device_id=peer, device_id_type=pl.DeviceIdType.MESH)
    pl.semaphore_wait(barrier, len(peers))

    direct(0)
    relay(0)
    direct(1)
    direct(2)
    for load in loads:
        load.wait()
    got(0, 4, 7, 8)

    def rotate(v, cosine, sine):
        return v * cosine + pltpu.roll(v, HD // 2, 1) * sine

    def unrotate(g, cosine, sine):
        return g * cosine + pltpu.roll(g * sine, HD // 2, 1)

    SHARD = 2 * TOK

    def project(slots):
        lo, hi = slots[0] * SHARD, (slots[-1] + 1) * SHARD
        at = [pl.ds(pl.multiple_of(((x + s - 1 + NX) % NX) * SHARD, SHARD), SHARD) for s in slots]
        for n in range(3):
            proj = mm(H[lo:hi, :], WI[:, n * 256 : n * 256 + 256]) * SCALE_IN
            for i, rows in enumerate(at):
                own = slice(i * SHARD, (i + 1) * SHARD)
                left, right = proj[own, :HD], proj[own, HD:]
                cosine, sine = COS[rows, :], SIN[rows, :]
                if n < 2:
                    Q[rows, n * 256 : n * 256 + HD] = rotate(left, cosine, sine).astype(BF16)
                    Q[rows, n * 256 + HD : n * 256 + 256] = rotate(right, cosine, sine).astype(BF16)
                else:
                    K[rows, :] = rotate(left, cosine, sine).astype(BF16)
                    V[rows, :] = right.astype(BF16)
        for s, rows in zip(slots, at):

            @pl.loop(0, D // 512)
            def _(n):
                c = pl.ds(pl.multiple_of(n * 512, 512), 512)
                HT[c, rows] = H[s * SHARD : (s + 1) * SHARD, c].T

    project((0, 1, 2))
    share(0)
    got(0, 9, 10)
    project((3,))
    relay(1)
    direct(3)

    RB = 128

    def forward(j):
        cols = pl.ds(pl.multiple_of(j * HD, HD), HD)
        for i in range(SEQ // RB):
            r, kx = i * RB, (i + 1) * RB
            s = mm_nt(Q[r : r + RB, cols], K[:kx, :]) * SCALE_HD
            row = lax.broadcasted_iota(jnp.int32, (RB, kx), 0) + r
            col = lax.broadcasted_iota(jnp.int32, (RB, kx), 1)
            s = jnp.where(row >= col, s, MASK_VALUE)
            e = jnp.exp(s - jnp.max(s, axis=1, keepdims=True))
            p = e * (1.0 / jnp.sum(e, axis=1, keepdims=True))
            PR[j, r : r + RB, :kx] = p
            c = mm(p.astype(BF16), V[:kx, :]).astype(BF16)
            C[r : r + RB, cols] = c
            CT[cols, r : r + RB] = c.T

    @pl.loop(0, HEADS)
    def _(j):
        forward(j)

        @pl.when(j == 1)
        def _():
            relay(2)
            direct(4)
            share(1)

    relay(3)
    share(2)

    def a_terms(p):
        for cols in part_cols(p):
            upstream = G[:, cols]
            weight = WO[:, cols]
            DA[...] += mm_nt(upstream, weight)
            grad = mm(CT[...], upstream)
            TA[:, cols] = (grad * G_OUT + weight.astype(F32) * W_SHARE).astype(BF16)

    def b_terms(p):
        for rows in part_cols(p):
            grad = mm(HT[rows, :], DP[...])
            TB[rows, :] = (grad * G_IN + WI[rows, :].astype(F32) * W_SHARE).astype(BF16)

    def length(n, e, sg):
        return n // 2 - (0 if (e == 0) == (sg == 1) else 1)

    def step(dist, n, e, sg, block, slots, ssems, rsems, dev):
        if dist > length(n, e, sg):
            return
        h = length(n, e, sg) - dist
        i = h + (0 if sg == 1 else length(n, e, 1))
        src = block
        if h > 0:
            src = slots.at[i - 1]
            remote(src, src, ssems.at[i - 1], rsems.at[i - 1], dev).wait_recv()
            src[...] = src[...] + block[...]
        remote(src, slots.at[i], ssems.at[i], rsems.at[i], dev).start()

    def total_at(n, e):
        return length(n, e, 1) - 1

    def last(n, e, block, slots, ssems, rsems, out=None):
        terms = [block[...].astype(F32)]
        for i in (total_at(n, e), n - 2):
            slot = slots.at[i]
            remote(slot, slot, ssems.at[i], rsems.at[i], sib).wait_recv()
            terms.append(slot[...].astype(F32))
        out = slots.at[total_at(n, e)] if out is None else out
        out[...] = (terms[0] + terms[1] + terms[2]).astype(BF16)

    def chunk_at(yt, zt):
        at = upper(yt) * (HALF_D - PAIR) + zt * PAIR + yt * CHUNK
        return pl.ds(pl.multiple_of(at, CHUNK), CHUNK)

    def pair_at(half, zt):
        return pl.ds(pl.multiple_of(half * HALF_D + zt * PAIR, PAIR), PAIR)

    WAYS = [(e, sg) for e in range(2) for sg in (1, -1)]

    def z_inside(k, piece, chunk, inner, i_s, i_r, outer, o_s, o_r, out):
        half = NZ // 2

        def inside(g):
            for i in range(half):

                @pl.when(k == i)
                def _(dist=half - i):
                    for e, sg in WAYS:
                        block = piece(e, pair_at(g, wrap(z + sg * dist, NZ)))
                        step(dist, NZ, e, sg, block, inner.at[e, g], i_s.at[e, g], i_r.at[e, g], z_dev(sg))

            @pl.when(k == half)
            def _():
                for e in range(2):
                    last(NZ, e, piece(e, pair_at(g, z)), inner.at[e, g], i_s.at[e, g], i_r.at[e, g])

        def chunk_of(e, yt):
            return chunk(inner.at[e, upper(yt), total_at(NZ, e)], yt - 2 * upper(yt))

        def outside():
            for dist in (2, 1):

                @pl.when(k == half + 2 - dist)
                def _(dist=dist):
                    for e, sg in WAYS:
                        block = chunk_of(e, wrap(y + sg * dist, NY))
                        step(dist, NY, e, sg, block, outer.at[e], o_s.at[e], o_r.at[e], y_dev(sg))

            @pl.when(k == half + 2)
            def _():
                for e in range(2):
                    last(NY, e, chunk_of(e, y), outer.at[e], o_s.at[e], o_r.at[e], out(e))

        return inside, outside

    def y_inside(k, piece, inner, i_s, i_r, outer, o_s, o_r, out):
        half = NZ // 2

        def one(dist, s, zt):
            for e, sg in WAYS:
                if dist > 0:
                    block = piece(e, chunk_at(wrap(y + sg * dist, NY), zt))
                    step(dist, NY, e, sg, block, inner.at[e, s], i_s.at[e, s], i_r.at[e, s], y_dev(sg))
                elif sg == 1:
                    last(NY, e, piece(e, chunk_at(y, zt)), inner.at[e, s], i_s.at[e, s], i_r.at[e, s])

        def inside(dist):
            g = k - (2 - dist)

            @pl.when((g >= 0) & (g <= half))
            def _():
                one(dist, half - g, wrap(z + half - g, NZ))

            @pl.when((g > 0) & (g < half))
            def _():
                one(dist, half + g, wrap(z - half + g, NZ))

        def outside():
            for dist in range(half, 0, -1):

                @pl.when(k == half + 2 - dist)
                def _(dist=dist):
                    for e, sg in WAYS:
                        block = inner.at[e, dist if sg == 1 else NZ - dist, total_at(NY, e)]
                        step(dist, NZ, e, sg, block, outer.at[e], o_s.at[e], o_r.at[e], z_dev(sg))

            @pl.when(k == half + 2)
            def _():
                for e in range(2):
                    block = inner.at[e, 0, total_at(NY, e)]
                    last(NZ, e, block, outer.at[e], o_s.at[e], o_r.at[e], out(e))

        return inside, outside

    def both(z_part, y_part):
        z_in, z_out = z_part
        y_in, y_out = y_part
        y_in(2)
        z_in(0)
        y_in(1)
        z_in(1)
        y_in(0)
        y_out()
        z_out()

    def lanes(ref, i):
        return ref.at[:, pl.ds(pl.multiple_of(i * CHUNK, CHUNK), CHUNK)]

    def sublanes(ref, i):
        return ref.at[pl.ds(pl.multiple_of(i * CHUNK, CHUNK), CHUNK)]

    def az_rows(d):
        return slice(d * A_ROWS, (d + 1) * A_ROWS)

    def ay_rows(d):
        return slice((2 + d) * A_ROWS, (3 + d) * A_ROWS)

    def bz_cols(d):
        return slice(d * BZ_COLS, (d + 1) * BZ_COLS)

    def by_cols(d):
        return slice(2 * BZ_COLS + d * BY_COLS, 2 * BZ_COLS + (d + 1) * BY_COLS)

    def a_round(k):
        z_part = z_inside(
            k, lambda d, at: TA.at[az_rows(d), at], lanes,
            az, az_s, az_r, azo, azo_s, azo_r, lambda d: sout_ref.at[az_rows(d)],
        )
        y_part = y_inside(
            k, lambda d, at: TA.at[ay_rows(d), at],
            ay, ay_s, ay_r, ayo, ayo_s, ayo_r, lambda d: sout_ref.at[ay_rows(d)],
        )
        both(z_part, y_part)

    def b_round(k):
        z_part = z_inside(
            k, lambda d, at: TB.at[at, bz_cols(d)], sublanes,
            bz, bz_s, bz_r, bzo, bzo_s, bzo_r, lambda d: sin_ref.at[:, bz_cols(d)],
        )
        y_part = y_inside(
            k, lambda d, at: TB.at[at, by_cols(d)],
            by, by_s, by_r, byo, byo_s, byo_r, lambda d: sin_ref.at[:, by_cols(d)],
        )
        both(z_part, y_part)

    PB = H

    def token_rows(xt, c):
        return pl.ds(pl.multiple_of((xt * 2 + c) * TOK, TOK), TOK)

    def sib_copy(i):
        return remote(PB.at[token_rows(i, 1 - core)], igr.at[i], sib_s.at[i], sib_r.at[i], sib)

    def x_step(h):
        if h == 0:
            for i in range(NX):
                sib_copy(i).wait_recv()
        for d in range(2):
            sg = 1 - 2 * d
            xt = (x - sg * (1 + h) + 2 * NX) % NX
            cols = slice(d * X_COLS, (d + 1) * X_COLS)
            term = PB[token_rows(xt, core), cols].astype(F32) + igr[xt, :, cols].astype(F32)
            if h == 0:
                x0[d] = term.astype(BF16)
                src = x0.at[d]
            else:
                src = xr.at[d, h - 1]
                remote(src, src, x_s.at[d, h - 1], x_r.at[d, h - 1], x_dev(sg)).wait_recv()
                total = (term + src[...].astype(F32)).astype(BF16)
                if h == NX - 1:
                    ig_ref[0, 0, :, cols] = total
                else:
                    src[...] = total
            if h < NX - 1:
                remote(src, xr.at[d, h], x_s.at[d, h], x_r.at[d, h], x_dev(sg)).start()

    def backward(heads):
        @pl.loop(*heads)
        def _(j):
            cols = pl.ds(pl.multiple_of(j * HD, HD), HD)
            for i in range(SEQ // RB):
                r, kx = i * RB, (i + 1) * RB
                dc = DC[r : r + RB, cols]
                p = PR[j, r : r + RB, :kx]
                delta = jnp.sum(
                    dc.astype(F32) * C[r : r + RB, cols].astype(F32), axis=1, keepdims=True
                )
                ds = (p * (mm_nt(dc, V[:kx, :]) - delta) * SCALE_HD).astype(BF16)
                DV[:kx, :] += mm_tn(p.astype(BF16), dc)
                DK[:kx, :] += mm_tn(ds, Q[r : r + RB, cols])
                g = mm(ds, K[:kx, :])
                turned = unrotate(g, COS[r : r + RB, :], SIN[r : r + RB, :])
                DP[r : r + RB, cols] = turned.astype(BF16)

    def backward_first():
        DC[...] = (DA[...] * SCALE_OUT).astype(BF16)
        backward((0, 2))

    def backward_last():
        backward((2, 4))
        DP[:, QW : QW + HD] = unrotate(DK[...], COS[...], SIN[...]).astype(BF16)
        DP[:, QW + HD :] = DV[...].astype(BF16)

    def input_terms(half):
        @pl.loop(half * (D // 512), (half + 1) * (D // 512))
        def _(n):
            at = pl.ds(pl.multiple_of(n * 256, 256), 256)
            PB[:, at] = (mm_nt(DP[...], WI[at, :]) * SCALE_IN).astype(BF16)

    def input_first():
        sent_all(0, 5, 6, 7, 8, 9, 10)
        input_terms(0)

    def input_last():
        input_terms(1)
        for i in range(NX):
            sib_copy(i).start()

    DA[...] = jnp.zeros_like(DA)
    DK[...] = jnp.zeros_like(DK)
    DV[...] = jnp.zeros_like(DV)

    LAG = 4
    ROUNDS = NY // 2 + NZ // 2 + 1

    got(1, 4, 7, 8, 9, 10)
    a_terms(0)

    @pl.loop(0, ROUNDS + LAG)
    def _(k):
        @pl.when(k < ROUNDS)
        def _():
            a_round(k)

        @pl.when(k >= LAG)
        def _():
            b_round(k - LAG)

        pl.when(k == 0)(functools.partial(share, 3))
        for p in range(1, 4):

            @pl.when(k == p - 1)
            def _(p=p):
                got(p + 1, 4, 7, 8, 9, 10)

        @pl.when(k < 3)
        def _():
            a_terms(k + 1)

        pl.when(k == 0)(functools.partial(relay, 4))
        pl.when(k == 1)(functools.partial(share, 4))
        pl.when(k == 3)(backward_first)
        pl.when(k == 3)(backward_last)

        @pl.when((k >= LAG - 1) & (k < LAG + 3))
        def _():
            b_terms(k - LAG + 1)

        pl.when(k == LAG)(input_first)
        pl.when(k == LAG + 1)(input_last)
        for h, at in enumerate((2, 3, 4, 6)):
            pl.when(k == LAG + at)(functools.partial(x_step, h))

    sent_all(0, 0, 1, 2, 3, 4)
    for i in range(1, 5):
        sent_all(i, *range(11))
    for i in range(NX):
        sib_copy(i).wait_send()

    def sent(slots, ssems, rsems):
        @pl.loop(0, ssems.shape[0])
        def _(h):
            remote(slots.at[h], slots.at[h], ssems.at[h], rsems.at[h], sib).wait_send()

    for d in range(2):
        sent(xr.at[d], x_s.at[d], x_r.at[d])
        for outer, o_s, o_r in ((azo, azo_s, azo_r), (ayo, ayo_s, ayo_r), (bzo, bzo_s, bzo_r), (byo, byo_s, byo_r)):
            sent(outer.at[d], o_s.at[d], o_r.at[d])
        for inner, i_s, i_r in ((az, az_s, az_r), (ay, ay_s, ay_r), (bz, bz_s, bz_r), (by, by_s, by_r)):

            @pl.loop(0, i_s.shape[1])
            def _(s):
                sent(inner.at[d, s], i_s.at[d, s], i_r.at[d, s])


def finish(a_ref, b_ref, c_ref, x_ref, y_ref, w_ref):
    x_ref[...] = a_ref[...]
    y_ref[...] = b_ref[...]
    w_ref[...] = c_ref[...]


def local(hidden_states, grad_output, w_in, w_out):
    cosine, sine = rope_tables()
    dma = pltpu.SemaphoreType.DMA
    scratch = [
        pltpu.VMEM((SEQ, D), BF16),
        pltpu.VMEM((SEQ, D), BF16),
        pltpu.VMEM((D, SEQ), BF16),
        pltpu.VMEM((D, IN_W), BF16),
        pltpu.VMEM((QW, D), BF16),
        pltpu.VMEM((QW, D), BF16),
        pltpu.VMEM((D, IN_W), BF16),
        pltpu.VMEM((SEQ, HD), F32),
        pltpu.VMEM((SEQ, HD), F32),
        pltpu.VMEM((SEQ, QW), BF16),
        pltpu.VMEM((SEQ, HD), BF16),
        pltpu.VMEM((SEQ, HD), BF16),
        pltpu.VMEM((HEADS, SEQ, SEQ), F32),
        pltpu.VMEM((SEQ, QW), BF16),
        pltpu.VMEM((QW, SEQ), BF16),
        pltpu.VMEM((SEQ, QW), BF16),
        pltpu.VMEM((SEQ, QW), F32),
        pltpu.VMEM((SEQ, IN_W), BF16),
        pltpu.VMEM((SEQ, HD), F32),
        pltpu.VMEM((SEQ, HD), F32),
        pltpu.VMEM((2, 2, NZ - 1, A_ROWS, PAIR), BF16),
        pltpu.VMEM((2, NY - 1, A_ROWS, CHUNK), BF16),
        pltpu.VMEM((2, NZ, NY - 1, A_ROWS, CHUNK), BF16),
        pltpu.VMEM((2, NZ - 1, A_ROWS, CHUNK), BF16),
        pltpu.VMEM((2, 2, NZ - 1, PAIR, BZ_COLS), BF16),
        pltpu.VMEM((2, NY - 1, CHUNK, BZ_COLS), BF16),
        pltpu.VMEM((2, NZ, NY - 1, CHUNK, BY_COLS), BF16),
        pltpu.VMEM((2, NZ - 1, CHUNK, BY_COLS), BF16),
        pltpu.VMEM((NX, TOK, D), BF16),
        pltpu.VMEM((2, TOK, X_COLS), BF16),
        pltpu.VMEM((2, NX - 1, TOK, X_COLS), BF16),
        dma((6,)),
        dma((5, 11)), dma((5, 11)),
    ]
    for _ in range(2):
        scratch += [dma((2, 2, NZ - 1))] * 2 + [dma((2, NY - 1))] * 2
        scratch += [dma((2, NZ, NY - 1))] * 2 + [dma((2, NZ - 1))] * 2
    scratch += [dma((NX,))] * 2 + [dma((2, NX - 1))] * 2
    hbm = pl.BlockSpec(memory_space=pl.ANY)
    vmem = pl.BlockSpec(memory_space=pltpu.VMEM)
    shapes = (
        jax.ShapeDtypeStruct((1, 1, TOK, D), BF16),
        jax.ShapeDtypeStruct((CHUNK, IN_W), BF16),
        jax.ShapeDtypeStruct((QW, CHUNK), BF16),
    )
    outs = pl.pallas_call(
        body,
        out_shape=shapes,
        in_specs=[hbm] * 6,
        out_specs=(vmem, vmem, vmem),
        scratch_shapes=scratch,
        compiler_params=pltpu.CompilerParams(
            collective_id=0, has_side_effects=True, vmem_limit_bytes=60 * 1024 * 1024
        ),
        cost_estimate=pl.CostEstimate(
            flops=16_000_000_000, bytes_accessed=12_000_000, transcendentals=1_000_000
        ),
    )(hidden_states, grad_output, w_in, w_out, jnp.asarray(cosine), jnp.asarray(sine))
    return pl.pallas_call(
        finish,
        out_shape=shapes,
        in_specs=[vmem] * 3,
        out_specs=(vmem, vmem, vmem),
    )(*outs)


def solution(mesh):
    in_specs = (
        P("replica", "dp", "tensor", None),
        P("replica", "dp", "tensor", None),
        P("replica", None, "tensor"),
        P("replica", "tensor", None),
    )
    out_specs = (
        P("replica", "dp", "tensor", None),
        P(("dp", "replica"), "tensor"),
        P("tensor", ("dp", "replica")),
    )
    return jax.shard_map(local, mesh=mesh, in_specs=in_specs, out_specs=out_specs, check_vma=False)
```
